32 devices in a mesh: group: 1, seq: 32 (over z, y, x, core).
Axes of the slice: x: 2, y: 2, z: 4, core: 2. Of those that a mesh axis runs over, the one named last changes fastest.
Arguments:
- enc_x: bfloat16 [256, 1280], P(('group', 'seq')), may hold values from -1.5 to 1.5
- enc_qkv: bfloat16 [256, 3, 640], P(('group', 'seq'))
- w_eo: bfloat16 [640, 1280], replicated, may hold values from -0.25 to 0.25
- w_kv: bfloat16 [1280, 2048], replicated, may hold values from -0.15625 to 0.15625
- dec_x: bfloat16 [32, 8192], P(('group', 'seq')), may hold values from -1.5 to 1.5
- w_q: bfloat16 [8192, 8192], P(None, 'seq'), may hold values from -0.0625 to 0.0625
- w_o: bfloat16 [8192, 8192], P(None, 'seq'), may hold values from -0.0625 to 0.0625
- cache_kv: bfloat16 [32, 4, 128, 2048], P(('group', 'seq'))
- doc_tile: int32 [32], P(('group', 'seq')), may hold values from 0 to 1
- cached_count: int32 [32], P(('group', 'seq')), may hold values from 0 to 3
Outputs:
- dec_out: bfloat16 [32, 8192], P(('group', 'seq'))
The draws below stay inside these ranges and needn't reach their ends.
All inputs are finite; a program needn't handle non-finite values.
Results may differ from the reference program's by a relative error of at most 0.017.
The reference program's roundings to bfloat16 on the way count: a program that leaves them out, or rounds other values in their place, can miss the bound.
Values may be sent and summed in bfloat16 or wider, within the bound.
No kernel may reach another device: no remote copies, remote signals or barrier semaphores. Data moves between devices by JAX's collectives and lax.ppermute only.
A program may use at most 64 MiB of HBM per device.

```python
import jax
import jax.numpy as jnp
from jax import lax

EW = 1280
EH = 8
EHD = 80
D = 8192
HD = 128
TILE_LEN = 128
SLOTS = 4
EA = 640
KVW = 1024
ETOK = 256
NEW_TILES = 2
DOCS = 32


def draw_enc_qkv(key, part):
    first = jax.random.fold_in(jax.random.fold_in(key, 11), 0)
    base = jax.random.normal(first, (ETOK, 3, EA), jnp.float32)
    which = jnp.arange(3).reshape(1, 3, 1) == 0
    scale = jnp.full((ETOK, 1, 1), 1.8, jnp.float32)
    base = base * jnp.where(which, scale, 1.0)
    return base.astype(jnp.bfloat16)


def draw_cache_kv(key, part):
    first = jax.random.fold_in(jax.random.fold_in(key, 23), 0)
    base = jax.random.normal(first, (DOCS, SLOTS, TILE_LEN, 2 * KVW), jnp.float32)
    return base.astype(jnp.bfloat16)


def with_ends(entries, own_key, least, top_value):
    spot = [jax.random.randint(jax.random.fold_in(own_key, axis), (), 0, length) for axis, length in enumerate(entries.shape)]
    longest = entries.shape.index(max(entries.shape))
    beside = spot[:longest] + [(spot[longest] + 1) % entries.shape[longest]] + spot[longest + 1:]
    return entries.at[tuple(spot)].set(least).at[tuple(beside)].set(top_value)


def level_of(key, dims, shards, smallest, top_value):
    loudness, own = 1.0, jax.random.fold_in(key, 6)
    for dim, parts in shards:
        heights = jnp.exp(jax.random.uniform(jax.random.fold_in(own, dim), (parts,), jnp.float32, smallest / len(shards), top_value / len(shards)))
        loudness = loudness * jnp.repeat(heights, dims[dim] // parts).reshape([-1 if axis == dim else 1 for axis in range(len(dims))])
    return loudness


def gaussian(own_key, dims, deviation, limit, cuts=(), kind=jnp.bfloat16):
    factor_of = level_of(own_key, dims, cuts, -0.22, 0.18) if cuts else 1.0
    drawn = jax.random.normal(own_key, dims, jnp.float32) * deviation * factor_of
    return jnp.minimum(jnp.maximum(drawn, -limit), limit).astype(kind)


def setup_inputs(seed: int = 0, part: int = 0) -> dict:
    seeds = jax.random.split(jax.random.key(seed), 11)
    part_keys = jax.random.split(jax.random.fold_in(seeds[10], part), 11)
    return {
        "enc_x": gaussian(part_keys[0], (ETOK, EW), 0.1, 1.5, ((0, 32),)),
        "enc_qkv": draw_enc_qkv(jax.random.fold_in(jax.random.fold_in(seeds[10], part), 71), part),
        "w_eo": gaussian(seeds[2], (EA, EW), EA ** -0.5, 0.25),
        "w_kv": gaussian(seeds[3], (EW, 2 * KVW), EW ** -0.5, 0.15625),
        "dec_x": gaussian(part_keys[4], (DOCS, D), 0.1, 1.5, ((0, 32),)),
        "w_q": gaussian(seeds[5], (D, D), D ** -0.5, 0.0625, ((1, 32),)),
        "w_o": gaussian(seeds[6], (D, D), D ** -0.5, 0.0625, ((1, 32),)),
        "cache_kv": draw_cache_kv(jax.random.fold_in(jax.random.fold_in(seeds[10], part), 71), part),
        "doc_tile": with_ends(jax.random.randint(part_keys[8], (DOCS,), 0, NEW_TILES), jax.random.fold_in(part_keys[8], 1), 0, NEW_TILES - 1).astype(jnp.int32),
        "cached_count": with_ends(jax.random.randint(part_keys[9], (DOCS,), 0, SLOTS), jax.random.fold_in(part_keys[9], 1), 0, SLOTS - 1).astype(jnp.int32),
    }


def layer_norm(values):
    center = values - lax.optimization_barrier(jnp.mean(values, axis=-1, keepdims=True))
    spread = lax.optimization_barrier(jnp.mean(center * center, axis=-1, keepdims=True))
    return center * lax.rsqrt(spread + 1e-05)

def doc_attend(query_row, doc_kv, filled):
    length = doc_kv.shape[0]
    width = doc_kv.shape[1] // 2
    kv_heads = width // HD
    query_heads = query_row.astype(jnp.float32).reshape(kv_heads, -1, HD)
    key_heads = doc_kv[:, :width].astype(jnp.float32).reshape(length, kv_heads, HD)
    value_heads = doc_kv[:, width:].astype(jnp.float32).reshape(length, kv_heads, HD)
    scores = jnp.einsum('gqd,kgd->gqk', query_heads, key_heads, precision=lax.Precision.HIGHEST) * HD ** (-0.5)
    inside = jnp.arange(length, dtype=jnp.int32) // TILE_LEN <= filled
    scores = jnp.where(inside[None, None, :], scores, -jnp.inf)
    weights = jax.nn.softmax(scores, axis=-1).astype(jnp.bfloat16).astype(jnp.float32)
    result = jnp.einsum('gqk,kgd->gqd', weights, value_heads, precision=lax.Precision.HIGHEST)
    return result.reshape(-1).astype(jnp.bfloat16)

def reference(enc_x, enc_qkv, w_eo, w_kv, dec_x, w_q, w_o, cache_kv, doc_tile, cached_count):
    query_all = enc_qkv[:, 0].reshape(ETOK, EH, EHD).transpose(1, 0, 2)
    key_all = enc_qkv[:, 1].reshape(ETOK, EH, EHD).transpose(1, 0, 2)
    value_all = enc_qkv[:, 2].reshape(ETOK, EH, EHD).transpose(1, 0, 2)

    def one_head(triple):
        query_head, key_head, value_head = triple
        scores = jnp.dot(query_head, key_head.T, preferred_element_type=jnp.float32) * EHD ** (-0.5)
        weights = jax.nn.softmax(scores, axis=-1).astype(jnp.bfloat16)
        return jnp.dot(weights, value_head, preferred_element_type=jnp.float32)
    heads_out = lax.map(one_head, (query_all, key_all, value_all))
    enc_attn = heads_out.transpose(1, 0, 2).reshape(ETOK, EA).astype(jnp.bfloat16)
    resid = enc_x.astype(jnp.float32) + jnp.dot(enc_attn, w_eo, preferred_element_type=jnp.float32)
    features = layer_norm(resid).astype(jnp.bfloat16)
    new_kv = jnp.dot(features, w_kv, preferred_element_type=jnp.float32).astype(jnp.bfloat16)
    tiles = new_kv.reshape(NEW_TILES, TILE_LEN, 2 * KVW)
    x_float = dec_x.astype(jnp.float32)
    normed = (x_float * lax.rsqrt(lax.optimization_barrier(jnp.mean(x_float * x_float, axis=-1, keepdims=True)) + 1e-05)).astype(jnp.bfloat16)
    queries = jnp.dot(normed, w_q, preferred_element_type=jnp.float32).astype(jnp.bfloat16)

    def one_doc(quad):
        query_row, cache_doc, tile_id, filled = quad
        chosen = lax.dynamic_index_in_dim(tiles, tile_id.astype(jnp.int32), 0, keepdims=True)
        zero = jnp.zeros((), jnp.int32)
        doc_kv = lax.dynamic_update_slice(cache_doc, chosen, (filled.astype(jnp.int32), zero, zero))
        return doc_attend(query_row, doc_kv.reshape(SLOTS * TILE_LEN, 2 * KVW), filled)
    dec_attn = lax.map(one_doc, (queries, cache_kv, doc_tile, cached_count))
    attn_out = jnp.dot(dec_attn, w_o, preferred_element_type=jnp.float32).astype(jnp.bfloat16)
    return (x_float + attn_out.astype(jnp.float32)).astype(jnp.bfloat16)
```

```python
import jax
import jax.numpy as jnp
from jax import lax
from jax.experimental import pallas as pl
from jax.experimental.pallas import tpu as pltpu
from jax.sharding import PartitionSpec as P

EH = 8
EHD = 80
HD = 128
TILE_LEN = 128
LANES = 128
SUB = 8
VMEM = pl.BlockSpec(memory_space=pltpu.VMEM)
SMEM = pl.BlockSpec(memory_space=pltpu.SMEM)
F32 = jnp.float32
BF16 = jnp.bfloat16


def params(mib):
    return pltpu.CompilerParams(vmem_limit_bytes=mib * 1024 * 1024)


def pack_kernel(dec_x_ref, qkv_ref, enc_x_ref, out_ref, rows_ref):
    x = dec_x_ref[...].astype(F32)
    scale = lax.rsqrt(jnp.mean(x * x, axis=-1, keepdims=True) + 1e-05)
    normed = x * scale
    groups = x.shape[1] // LANES
    for k in range(groups):
        rows_ref[k : k + 1, :] = normed[:, k * LANES : (k + 1) * LANES]
    copies = out_ref.shape[0]

    def put(place, block):
        block = block.astype(BF16)
        for copy in range(copies):
            out_ref[copy, place] = block

    for i in range(groups // SUB):
        put(i, rows_ref[i * SUB : (i + 1) * SUB, :])
    place = groups // SUB
    qkv = qkv_ref[...].astype(F32)
    for i in range(3):
        part = qkv[:, i, :]
        for t in range(part.shape[1] // LANES):
            put(place, part[:, t * LANES : (t + 1) * LANES])
            place += 1
    enc_x = enc_x_ref[...]
    for t in range(enc_x.shape[1] // LANES):
        put(place, enc_x[:, t * LANES : (t + 1) * LANES])
        place += 1


def project_kernel(own_ref, other_ref, w_ref, out_ref, rows_ref, x_ref):
    chips = own_ref.shape[0]
    depth = w_ref.shape[0]
    for side, ref in enumerate((own_ref, other_ref)):
        for i in range(depth // (SUB * LANES)):
            rows_ref[...] = ref[:, i].astype(F32).reshape(chips * SUB, LANES)
            for j in range(SUB):
                k = i * SUB + j
                x_ref[side * chips : (side + 1) * chips, k * LANES : (k + 1) * LANES] = rows_ref[
                    pl.ds(j, chips, stride=SUB), :
                ].astype(BF16)
    result = jnp.dot(x_ref[...], w_ref[...], preferred_element_type=F32)
    core = lax.rem(lax.axis_index("seq"), 2)
    parts, lanes = out_ref.shape[2:]
    for side in range(2):
        half = result[side * chips : (side + 1) * chips]
        half = jnp.stack([half[:, p * lanes : (p + 1) * lanes] for p in range(parts)], axis=1)
        where = core if side == 0 else 1 - core
        out_ref[:, pl.ds(where, 1)] = half.astype(BF16)[:, None]


def encode_kernel(tile_ref, own_ref, other_ref, w_eo_ref, w_kv_ref, out_ref):
    width = w_eo_ref.shape[0]
    model = w_eo_ref.shape[1]
    tiles = width // LANES
    first = own_ref.shape[1] - 3 * tiles - model // LANES
    chips = TILE_LEN // (2 * SUB)
    mine = pl.ds(tile_ref[0] * chips, chips)

    def merge(block):
        return block.astype(F32).reshape(-1, LANES)

    def every(place):
        return jnp.concatenate([merge(own_ref[:, place]), merge(other_ref[:, place])], axis=0).astype(BF16)

    def tile_rows(place):
        return jnp.concatenate([merge(own_ref[mine, place]), merge(other_ref[mine, place])], axis=0)

    query = jnp.concatenate([tile_rows(first + t) for t in range(tiles)], axis=1).astype(BF16)
    keys = jnp.concatenate([every(first + tiles + t) for t in range(tiles)], axis=1)
    values = jnp.concatenate([every(first + 2 * tiles + t) for t in range(tiles)], axis=1)
    column = lax.broadcasted_iota(jnp.int32, (TILE_LEN, width), 1)
    attn = [jnp.zeros((TILE_LEN, LANES), F32) for _ in range(tiles)]
    for h in range(EH):
        lo, hi = h * EHD // LANES, (h * EHD + EHD - 1) // LANES + 1
        span = slice(lo * LANES, hi * LANES)
        inside = (column[:, span] >= h * EHD) & (column[:, span] < (h + 1) * EHD)
        head = jnp.where(inside, query[:, span], jnp.zeros((), BF16))
        scores = lax.dot_general(head, keys[:, span], (((1,), (1,)), ((), ())), preferred_element_type=F32)
        scores = scores * EHD ** (-0.5)
        powers = jnp.exp(scores - jnp.max(scores, axis=-1, keepdims=True))
        weights = (powers / jnp.sum(powers, axis=-1, keepdims=True)).astype(BF16)
        part = jnp.dot(weights, values[:, span], preferred_element_type=F32)
        part = jnp.where(inside, part, 0.0)
        for t in range(lo, hi):
            attn[t] = attn[t] + part[:, (t - lo) * LANES : (t - lo + 1) * LANES]
    attn = jnp.concatenate(attn, axis=1).astype(BF16)
    enc_x = jnp.concatenate([tile_rows(first + 3 * tiles + t) for t in range(model // LANES)], axis=1)
    resid = enc_x + jnp.dot(attn, w_eo_ref[...], preferred_element_type=F32)
    center = resid - jnp.mean(resid, axis=-1, keepdims=True)
    spread = jnp.mean(center * center, axis=-1, keepdims=True)
    features = (center * lax.rsqrt(spread + 1e-05)).astype(BF16)
    out_ref[...] = jnp.dot(features, w_kv_ref[...], preferred_element_type=F32).astype(BF16)


def attend_kernel(count_ref, query_ref, cache_ref, new_ref, out_ref):
    filled = count_ref[0]
    slots, length, both = cache_ref.shape[1:]
    width = both // 2
    kv_heads = width // HD
    per = query_ref.shape[0] // kv_heads
    query = query_ref[...]
    scores = []
    for g in range(kv_heads):
        head = query[g * per : (g + 1) * per]
        cols = slice(g * HD, (g + 1) * HD)
        keys = cache_ref[0, :, :, cols].reshape(slots * length, HD)
        old = lax.dot_general(head, keys, (((1,), (1,)), ((), ())), preferred_element_type=F32)
        new = lax.dot_general(head, new_ref[:, cols], (((1,), (1,)), ((), ())), preferred_element_type=F32)
        scores.append(jnp.concatenate([old, new], axis=1))
    scores = jnp.concatenate(scores, axis=0) * HD ** (-0.5)
    slot = lax.broadcasted_iota(jnp.int32, scores.shape, 1) // length
    scores = jnp.where((slot < filled) | (slot == slots), scores, -jnp.inf)
    powers = jnp.exp(scores - jnp.max(scores, axis=-1, keepdims=True))
    weights = (powers / jnp.sum(powers, axis=-1, keepdims=True)).astype(BF16)
    copies = out_ref.shape[0]
    for g in range(kv_heads):
        mine = weights[g * per : (g + 1) * per]
        cols = slice(width + g * HD, width + (g + 1) * HD)
        values = cache_ref[0, :, :, cols].reshape(slots * length, HD)
        part = jnp.dot(mine[:, : slots * length], values, preferred_element_type=F32)
        part = part + jnp.dot(mine[:, slots * length :], new_ref[:, cols], preferred_element_type=F32)
        part = part.astype(BF16)
        for copy in range(copies):
            out_ref[copy, g] = part


def finish_kernel(attn_ref, dec_x_ref, out_ref):
    attn = attn_ref[...].astype(F32)
    for k in range(attn.shape[0]):
        cols = slice(k * LANES, (k + 1) * LANES)
        out_ref[:, cols] = (dec_x_ref[:, cols].astype(F32) + attn[k : k + 1]).astype(BF16)


def solution(mesh):
    devices = mesh.shape["seq"]
    chips = devices // 2
    across = [[2 * chip + core for chip in range(chips)] for core in range(2)]
    swap = [(i, i ^ 1) for i in range(devices)]

    def gather(copies):
        own = lax.all_to_all(copies, "seq", 0, 0, tiled=True, axis_index_groups=across)
        return own, lax.ppermute(own, "seq", swap)

    def project(own, other, weight):
        depth, cols = weight.shape
        lanes = min(cols, LANES)
        out = pl.pallas_call(
            project_kernel,
            out_shape=jax.ShapeDtypeStruct((chips, 2, cols // lanes, lanes), BF16),
            in_specs=[VMEM] * 3,
            out_specs=VMEM,
            scratch_shapes=[pltpu.VMEM((chips * SUB, LANES), F32), pltpu.VMEM((2 * chips, depth), BF16)],
            compiler_params=params(24),
        )(own, other, weight)
        sent = out.reshape(devices, cols // lanes, lanes)
        return lax.all_to_all(sent, "seq", 0, 0, tiled=True).reshape(-1, LANES)

    def local(enc_x, enc_qkv, w_eo, w_kv, dec_x, w_q, w_o, cache_kv, doc_tile, cached_count):
        groups = (dec_x.size + enc_qkv.size + enc_x.size) // (SUB * LANES)
        packed = pl.pallas_call(
            pack_kernel,
            out_shape=jax.ShapeDtypeStruct((chips, groups, SUB, LANES), BF16),
            in_specs=[VMEM] * 3,
            out_specs=VMEM,
            scratch_shapes=[pltpu.VMEM((dec_x.shape[1] // LANES, LANES), F32)],
            compiler_params=params(16),
        )(dec_x, enc_qkv, enc_x)
        own, other = gather(packed)
        query = project(own, other, w_q)
        new_kv = pl.pallas_call(
            encode_kernel,
            out_shape=jax.ShapeDtypeStruct((TILE_LEN, w_kv.shape[1]), BF16),
            in_specs=[SMEM] + [VMEM] * 4,
            out_specs=VMEM,
            compiler_params=params(40),
        )(doc_tile, own, other, w_eo, w_kv)
        heads = query.shape[0]
        copies = pl.pallas_call(
            attend_kernel,
            out_shape=jax.ShapeDtypeStruct((chips, heads // SUB, SUB, LANES), BF16),
            in_specs=[SMEM] + [VMEM] * 3,
            out_specs=VMEM,
            compiler_params=params(24),
        )(cached_count, query, cache_kv, new_kv)
        own, other = gather(copies)
        attn_out = project(own, other, w_o)
        return pl.pallas_call(
            finish_kernel,
            out_shape=jax.ShapeDtypeStruct(dec_x.shape, BF16),
            in_specs=[VMEM] * 2,
            out_specs=VMEM,
            compiler_params=params(16),
        )(attn_out, dec_x)

    return jax.shard_map(
        local,
        mesh=mesh,
        in_specs=(
            P(("group", "seq"), None),
            P(("group", "seq"), None, None),
            P(),
            P(),
            P(("group", "seq"), None),
            P(None, "seq"),
            P(None, "seq"),
            P(("group", "seq"), None, None, None),
            P(("group", "seq")),
            P(("group", "seq")),
        ),
        out_specs=P(("group", "seq"), None),
        check_vma=False,
    )
```

```python
import jax
import jax.numpy as jnp
from jax import lax
from jax.experimental import pallas as pl
from jax.experimental.pallas import tpu as pltpu
from jax.sharding import PartitionSpec as P

EH = 8
EHD = 80
HD = 128
TILE_LEN = 128
LANES = 128
SUB = 8
SHARES = 4
VMEM = pl.BlockSpec(memory_space=pltpu.VMEM)
ANY = pl.BlockSpec(memory_space=pl.ANY)
SMEM = pl.BlockSpec(memory_space=pltpu.SMEM)
LONG = pl.CostEstimate(flops=10**10, transcendentals=0, bytes_accessed=10**7)
F32 = jnp.float32
BF16 = jnp.bfloat16


def params(mib):
    return pltpu.CompilerParams(vmem_limit_bytes=mib * 1024 * 1024)


def pack_kernel(dec_x_hbm, qkv_hbm, enc_x_hbm, out_ref, dec_x_ref, qkv_ref, enc_x_ref, rows_ref, sems):
    copies = [
        pltpu.make_async_copy(src, dst, sems.at[i])
        for i, (src, dst) in enumerate(((dec_x_hbm, dec_x_ref), (qkv_hbm, qkv_ref), (enc_x_hbm, enc_x_ref)))
    ]
    for copy in copies:
        copy.start()
    for copy in copies:
        copy.wait()
    x = dec_x_ref[...].astype(F32)
    scale = lax.rsqrt(jnp.mean(x * x, axis=-1, keepdims=True) + 1e-05)
    normed = x * scale
    groups = x.shape[1] // LANES
    for k in range(groups):
        rows_ref[k : k + 1, :] = normed[:, k * LANES : (k + 1) * LANES]
    copies = out_ref.shape[0]

    def put(place, block, to):
        block = block.astype(BF16)
        for copy in to:
            out_ref[copy, place] = block

    for i in range(groups // SUB):
        put(i, rows_ref[i * SUB : (i + 1) * SUB, :], range(copies))
    blocks = []
    for i in range(3):
        part = qkv_ref[i]
        blocks += [part[:, t * LANES : (t + 1) * LANES] for t in range(part.shape[1] // LANES)]
    enc_x = enc_x_ref[...]
    blocks += [enc_x[:, t * LANES : (t + 1) * LANES] for t in range(enc_x.shape[1] // LANES)]
    share = len(blocks) // SHARES
    first = groups // SUB
    for i, block in enumerate(blocks[share * SHARES :]):
        put(first + i, block, range(copies))
    first = out_ref.shape[1] - share
    for i, block in enumerate(blocks[: share * SHARES]):
        put(first + i % share, block, range(i // share, copies, SHARES))


def regroup(ref, rows_ref, x_ref):
    chips = ref.shape[0]
    for i in range(x_ref.shape[1] // (SUB * LANES)):
        rows_ref[...] = ref[:, i].astype(F32).reshape(chips * SUB, LANES)
        for j in range(SUB):
            k = i * SUB + j
            x_ref[:, k * LANES : (k + 1) * LANES] = rows_ref[pl.ds(j, chips, stride=SUB), :].astype(BF16)


def own_kernel(own_ref, w_ref, result_ref, rows_ref, x_ref):
    regroup(own_ref, rows_ref, x_ref)
    result_ref[...] = jnp.dot(x_ref[...], w_ref[...], preferred_element_type=F32)


def other_kernel(other_ref, result_ref, w_ref, out_ref, rows_ref, x_ref):
    regroup(other_ref, rows_ref, x_ref)
    result = jnp.dot(x_ref[...], w_ref[...], preferred_element_type=F32)
    core = lax.rem(lax.axis_index("seq"), 2)
    parts, lanes = out_ref.shape[2:]
    for half, where in ((result_ref[...], core), (result, 1 - core)):
        half = jnp.stack([half[:, p * lanes : (p + 1) * lanes] for p in range(parts)], axis=1)
        out_ref[:, pl.ds(where, 1)] = half.astype(BF16)[:, None]


def share_kernel(own_ref, out_ref):
    share = out_ref.shape[1]
    out_ref[...] = own_ref[:, own_ref.shape[1] - share :]


def pass_kernel(query_ref, out_ref):
    out_ref[...] = query_ref[...]


def merge_kernel(query_ref, own_ref, own_1, own_2, own_3, out_ref):
    share = own_1.shape[1]
    last = own_ref.shape[1] - share
    place = lax.rem(lax.axis_index("seq") // 2, SHARES)

    def merge(block):
        return block.astype(F32).reshape(-1, LANES).astype(BF16)

    for j, ref in enumerate((own_ref, own_1, own_2, own_3)):
        start = jnp.bitwise_xor(place, j) * share
        for i in range(share):
            out_ref[start + i] = merge(ref[:, (last if j == 0 else 0) + i])
    for i in range(out_ref.shape[0] - share * SHARES):
        out_ref[share * SHARES + i] = merge(own_ref[:, last - 1 - i])


def encode_kernel(tile_ref, own_ref, other_ref, w_eo_ref, w_kv_ref, out_ref):
    width = w_eo_ref.shape[0]
    model = w_eo_ref.shape[1]
    tiles = width // LANES
    half = TILE_LEN // 2
    start = pl.multiple_of(tile_ref[0] * half, half)

    def tile_rows(place):
        return jnp.concatenate([own_ref[place, pl.ds(start, half)], other_ref[place, pl.ds(start, half)]], axis=0)

    def every(place):
        return jnp.concatenate([own_ref[place], other_ref[place]], axis=0)

    query = jnp.concatenate([tile_rows(t) for t in range(tiles)], axis=1)
    keys = jnp.concatenate([every(tiles + t) for t in range(tiles)], axis=1)
    values = jnp.concatenate([every(2 * tiles + t) for t in range(tiles)], axis=1)
    column = lax.broadcasted_iota(jnp.int32, (TILE_LEN, width), 1)
    attn = [jnp.zeros((TILE_LEN, LANES), F32) for _ in range(tiles)]
    for h in range(EH):
        lo, hi = h * EHD // LANES, (h * EHD + EHD - 1) // LANES + 1
        span = slice(lo * LANES, hi * LANES)
        inside = (column[:, span] >= h * EHD) & (column[:, span] < (h + 1) * EHD)
        head = jnp.where(inside, query[:, span], jnp.zeros((), BF16))
        scores = lax.dot_general(head, keys[:, span], (((1,), (1,)), ((), ())), preferred_element_type=F32)
        scores = scores * EHD ** (-0.5)
        powers = jnp.exp(scores - jnp.max(scores, axis=-1, keepdims=True))
        weights = (powers / jnp.sum(powers, axis=-1, keepdims=True)).astype(BF16)
        part = jnp.dot(weights, values[:, span], preferred_element_type=F32)
        part = jnp.where(inside, part, 0.0)
        for t in range(lo, hi):
            attn[t] = attn[t] + part[:, (t - lo) * LANES : (t - lo + 1) * LANES]
    attn = jnp.concatenate(attn, axis=1).astype(BF16)
    enc_x = jnp.concatenate([tile_rows(3 * tiles + t).astype(F32) for t in range(model // LANES)], axis=1)
    resid = enc_x + jnp.dot(attn, w_eo_ref[...], preferred_element_type=F32)
    center = resid - jnp.mean(resid, axis=-1, keepdims=True)
    spread = jnp.mean(center * center, axis=-1, keepdims=True)
    features = (center * lax.rsqrt(spread + 1e-05)).astype(BF16)
    out_ref[...] = jnp.dot(features, w_kv_ref[...], preferred_element_type=F32).astype(BF16)


def attend_kernel(count_ref, query_ref, cache_ref, new_ref, out_ref):
    filled = count_ref[0]
    slots, length, both = cache_ref.shape
    width = both // 2
    kv_heads = width // HD
    per = query_ref.shape[0] // kv_heads
    query = query_ref[...]
    scores = []
    for g in range(kv_heads):
        head = query[g * per : (g + 1) * per]
        cols = slice(g * HD, (g + 1) * HD)
        keys = cache_ref[:, :, cols].reshape(slots * length, HD)
        old = lax.dot_general(head, keys, (((1,), (1,)), ((), ())), preferred_element_type=F32)
        new = lax.dot_general(head, new_ref[:, cols], (((1,), (1,)), ((), ())), preferred_element_type=F32)
        scores.append(jnp.concatenate([old, new], axis=1))
    scores = jnp.concatenate(scores, axis=0) * HD ** (-0.5)
    slot = lax.broadcasted_iota(jnp.int32, scores.shape, 1) // length
    scores = jnp.where((slot < filled) | (slot == slots), scores, -jnp.inf)
    powers = jnp.exp(scores - jnp.max(scores, axis=-1, keepdims=True))
    weights = (powers / jnp.sum(powers, axis=-1, keepdims=True)).astype(BF16)
    copies = out_ref.shape[0]
    for g in range(kv_heads):
        mine = weights[g * per : (g + 1) * per]
        cols = slice(width + g * HD, width + (g + 1) * HD)
        values = cache_ref[:, :, cols].reshape(slots * length, HD)
        part = jnp.dot(mine[:, : slots * length], values, preferred_element_type=F32)
        part = part + jnp.dot(mine[:, slots * length :], new_ref[:, cols], preferred_element_type=F32)
        part = part.astype(BF16)
        for copy in range(copies):
            out_ref[copy, g] = part


def finish_kernel(attn_ref, dec_x_ref, out_ref):
    attn = attn_ref[...].astype(F32)
    for k in range(attn.shape[0]):
        cols = slice(k * LANES, (k + 1) * LANES)
        out_ref[:, cols] = (dec_x_ref[:, cols].astype(F32) + attn[k : k + 1]).astype(BF16)


def solution(mesh):
    devices = mesh.shape["seq"]
    chips = devices // 2
    across = [[2 * chip + core for chip in range(chips)] for core in range(2)]
    swap = [(i, i ^ 1) for i in range(devices)]

    def gather(copies):
        own = lax.all_to_all(copies, "seq", 0, 0, tiled=True, axis_index_groups=across)
        return own, lax.ppermute(own, "seq", swap)

    def project(own, other, weight):
        depth, cols = weight.shape
        lanes = min(cols, LANES)
        scratch = [pltpu.VMEM((chips * SUB, LANES), F32), pltpu.VMEM((chips, depth), BF16)]
        result = pl.pallas_call(
            own_kernel,
            out_shape=jax.ShapeDtypeStruct((chips, cols), F32),
            in_specs=[VMEM, VMEM],
            out_specs=VMEM,
            scratch_shapes=scratch,
            compiler_params=params(4),
            cost_estimate=LONG,
        )(own, weight)
        out = pl.pallas_call(
            other_kernel,
            out_shape=jax.ShapeDtypeStruct((chips, 2, cols // lanes, lanes), BF16),
            in_specs=[VMEM] * 3,
            out_specs=VMEM,
            scratch_shapes=scratch,
            compiler_params=params(4),
            cost_estimate=LONG,
        )(other, result, weight)
        sent = out.reshape(devices, cols // lanes, lanes)
        return lax.all_to_all(sent, "seq", 0, 0, tiled=True).reshape(-1, LANES)

    def local(enc_x, enc_qkv, w_eo, w_kv, dec_x, w_q, w_o, cache_kv, doc_tile, cached_count):
        qkv = enc_qkv.transpose(1, 0, 2)
        blocks = (enc_qkv.size + enc_x.size) // (SUB * LANES)
        share = blocks // SHARES
        groups = dec_x.size // (SUB * LANES) + blocks - share * (SHARES - 1)
        packed = pl.pallas_call(
            pack_kernel,
            out_shape=jax.ShapeDtypeStruct((chips, groups, SUB, LANES), BF16),
            in_specs=[ANY] * 3,
            out_specs=VMEM,
            scratch_shapes=[
                pltpu.VMEM(dec_x.shape, BF16),
                pltpu.VMEM(qkv.shape, BF16),
                pltpu.VMEM(enc_x.shape, BF16),
                pltpu.VMEM((dec_x.shape[1] // LANES, LANES), F32),
                pltpu.SemaphoreType.DMA((3,)),
            ],
            compiler_params=params(56),
            cost_estimate=LONG,
        )(dec_x, qkv, enc_x)
        own, other = gather(packed)
        mine = pl.pallas_call(
            share_kernel,
            out_shape=jax.ShapeDtypeStruct((chips, share, SUB, LANES), BF16),
            in_specs=[VMEM],
            out_specs=VMEM,
            compiler_params=params(1),
        )(own)
        shares = [lax.ppermute(mine, "seq", [(i, i ^ (2 * j)) for i in range(devices)]) for j in range(1, SHARES)]
        query = project(own, other, w_q)
        query = pl.pallas_call(
            pass_kernel,
            out_shape=jax.ShapeDtypeStruct(query.shape, BF16),
            in_specs=[VMEM],
            out_specs=VMEM,
            compiler_params=params(1),
        )(query)
        merged = pl.pallas_call(
            merge_kernel,
            out_shape=jax.ShapeDtypeStruct((blocks, chips * SUB, LANES), BF16),
            in_specs=[VMEM] * 5,
            out_specs=VMEM,
            compiler_params=params(2),
            cost_estimate=LONG,
        )(query, own, *shares)
        new_kv = pl.pallas_call(
            encode_kernel,
            out_shape=jax.ShapeDtypeStruct((TILE_LEN, w_kv.shape[1]), BF16),
            in_specs=[SMEM] + [VMEM] * 4,
            out_specs=VMEM,
            compiler_params=params(12),
            cost_estimate=LONG,
        )(doc_tile, merged, lax.ppermute(merged, "seq", swap), w_eo, w_kv)
        heads = query.shape[0]
        copies = pl.pallas_call(
            attend_kernel,
            out_shape=jax.ShapeDtypeStruct((chips, heads // SUB, SUB, LANES), BF16),
            in_specs=[SMEM] + [VMEM] * 3,
            out_specs=VMEM,
            compiler_params=params(4),
            cost_estimate=LONG,
        )(cached_count, query, cache_kv[0], new_kv)
        own, other = gather(copies)
        attn_out = project(own, other, w_o)
        return pl.pallas_call(
            finish_kernel,
            out_shape=jax.ShapeDtypeStruct(dec_x.shape, BF16),
            in_specs=[VMEM] * 2,
            out_specs=VMEM,
            compiler_params=params(2),
            cost_estimate=LONG,
        )(attn_out, dec_x)

    return jax.shard_map(
        local,
        mesh=mesh,
        in_specs=(
            P(("group", "seq"), None),
            P(("group", "seq"), None, None),
            P(),
            P(),
            P(("group", "seq"), None),
            P(None, "seq"),
            P(None, "seq"),
            P(("group", "seq"), None, None, None),
            P(("group", "seq")),
            P(("group", "seq")),
        ),
        out_specs=P(("group", "seq"), None),
        check_vma=False,
    )
```

```python
import functools

import jax
import jax.numpy as jnp
from jax import lax
from jax.experimental import pallas as pl
from jax.experimental.pallas import tpu as pltpu
from jax.sharding import PartitionSpec as P

EH = 8
EHD = 80
HD = 128
TILE_LEN = 128
LANES = 128
SUB = 8
SHARES = 4
CHUNK = 512
VMEM = pl.BlockSpec(memory_space=pltpu.VMEM)
ANY = pl.BlockSpec(memory_space=pl.ANY)
SMEM = pl.BlockSpec(memory_space=pltpu.SMEM)
LONG = pl.CostEstimate(flops=10**10, transcendentals=0, bytes_accessed=10**7)
F32 = jnp.float32
BF16 = jnp.bfloat16


def params(mib):
    return pltpu.CompilerParams(vmem_limit_bytes=mib * 1024 * 1024)


def pack_kernel(dec_x_hbm, qkv_hbm, enc_x_hbm, out_ref, dec_x_ref, qkv_ref, enc_x_ref, rows_ref, sems):
    copies = [
        pltpu.make_async_copy(src, dst, sems.at[i])
        for i, (src, dst) in enumerate(((dec_x_hbm, dec_x_ref), (qkv_hbm, qkv_ref), (enc_x_hbm, enc_x_ref)))
    ]
    for copy in copies:
        copy.start()
    for copy in copies:
        copy.wait()
    x = dec_x_ref[...].astype(F32)
    scale = lax.rsqrt(jnp.mean(x * x, axis=-1, keepdims=True) + 1e-05)
    normed = x * scale
    groups = x.shape[1] // LANES
    for k in range(groups):
        rows_ref[k : k + 1, :] = normed[:, k * LANES : (k + 1) * LANES]
    copies = out_ref.shape[0]

    def put(place, block, to):
        block = block.astype(BF16)
        for copy in to:
            out_ref[copy, place] = block

    halves = groups // SUB // 2
    for i in range(2 * halves):
        put(i % halves, rows_ref[i * SUB : (i + 1) * SUB, :], range(i // halves, copies, 2))
    blocks = []
    for i in range(3):
        part = qkv_ref[i]
        blocks += [part[:, t * LANES : (t + 1) * LANES] for t in range(part.shape[1] // LANES)]
    enc_x = enc_x_ref[...]
    blocks += [enc_x[:, t * LANES : (t + 1) * LANES] for t in range(enc_x.shape[1] // LANES)]
    share = len(blocks) // (2 * SHARES)
    for i, block in enumerate(blocks[2 * SHARES * share :]):
        put(halves + i, block, range(copies))
    first = out_ref.shape[1] - share
    for i, block in enumerate(blocks[: 2 * SHARES * share]):
        core, chip = divmod(i // share, SHARES)
        put(first + i % share, block, range(2 * chip + core, copies, 2 * SHARES))


def project_kernel(sent_ref, w_ref, mate_ref, *refs):
    out_ref, rows_ref, x_ref = refs[-3:]
    docs, half = x_ref.shape
    for i in range(half // (SUB * LANES)):
        rows_ref[...] = sent_ref[:, i].astype(F32).reshape(docs * SUB, LANES)
        for j in range(SUB):
            k = i * SUB + j
            x_ref[:, k * LANES : (k + 1) * LANES] = rows_ref[pl.ds(j, docs, stride=SUB), :].astype(BF16)
    core = lax.rem(lax.axis_index("seq"), 2)
    parts, lanes = out_ref.shape[2:]

    def multiply(side):
        for ref, place in ((w_ref, side), (mate_ref, 1 - side)):
            result = jnp.zeros((docs, ref.shape[1]), F32)
            for k in range(0, half, CHUNK):
                rows = slice(side * half + k, side * half + k + CHUNK)
                result += jnp.dot(x_ref[:, k : k + CHUNK], ref[rows, :], preferred_element_type=F32)
            result = jnp.stack([result[:, p * lanes : (p + 1) * lanes] for p in range(parts)], axis=1)
            out_ref[:, place] = result

    for side in range(2):
        pl.when(core == side)(functools.partial(multiply, side))


def add_halves(sums_ref, rows_ref):
    devices, cores, parts, _ = sums_ref.shape
    for chip in range(devices // 2):
        for core in range(cores):
            row = (chip * cores + core) * parts
            rows_ref[row : row + parts, :] = sums_ref[2 * chip, core] + sums_ref[2 * chip + 1, core]
    return rows_ref[...].astype(BF16)


def collect_kernel(sums_ref, out_ref, rows_ref):
    out_ref[...] = add_halves(sums_ref, rows_ref)


def share_kernel(own_ref, out_ref):
    share = out_ref.shape[1]
    out_ref[...] = own_ref[:, own_ref.shape[1] - share :]


def merge(block):
    return block.astype(F32).reshape(-1, LANES).astype(BF16)


def merge_kernel(query_ref, own_0, own_1, own_2, own_3, out_ref):
    share = own_0.shape[1]
    place = lax.rem(lax.axis_index("seq") // 2, SHARES)
    for j, ref in enumerate((own_0, own_1, own_2, own_3)):
        start = jnp.bitwise_xor(place, j) * share
        for i in range(share):
            out_ref[start + i] = merge(ref[:, i])


def encode_kernel(tile_ref, sent_ref, own_ref, other_ref, w_eo_ref, w_kv_ref, out_ref):
    width, model = w_eo_ref.shape
    tiles = width // LANES
    held = own_ref.shape[0]
    rest = 3 * tiles + model // LANES - 2 * held
    first = sent_ref.shape[1] - held // SHARES - rest
    core = lax.rem(lax.axis_index("seq"), 2)
    mine = pl.ds(pl.multiple_of(tile_ref[0] * TILE_LEN, TILE_LEN), TILE_LEN)

    def pick(place, rows):
        if place >= 2 * held:
            chunk = TILE_LEN // SUB
            block = sent_ref[pl.ds(tile_ref[0] * chunk, chunk), first + place - 2 * held]
            return merge(block)
        side, index = divmod(place, held)
        return jnp.where(core == side, own_ref[index, rows], other_ref[index, rows])

    every = slice(None)
    query = jnp.concatenate([pick(t, mine) for t in range(tiles)], axis=1)
    keys = jnp.concatenate([pick(tiles + t, every) for t in range(tiles)], axis=1)
    values = jnp.concatenate([pick(2 * tiles + t, every) for t in range(tiles)], axis=1)
    column = lax.broadcasted_iota(jnp.int32, (TILE_LEN, width), 1)
    attn = [jnp.zeros((TILE_LEN, LANES), F32) for _ in range(tiles)]
    for h in range(EH):
        lo, hi = h * EHD // LANES, (h * EHD + EHD - 1) // LANES + 1
        span = slice(lo * LANES, hi * LANES)
        inside = (column[:, span] >= h * EHD) & (column[:, span] < (h + 1) * EHD)
        head = jnp.where(inside, query[:, span], jnp.zeros((), BF16))
        scores = lax.dot_general(head, keys[:, span], (((1,), (1,)), ((), ())), preferred_element_type=F32)
        scores = scores * EHD ** (-0.5)
        powers = jnp.exp(scores - jnp.max(scores, axis=-1, keepdims=True))
        weights = (powers / jnp.sum(powers, axis=-1, keepdims=True)).astype(BF16)
        part = jnp.dot(weights, values[:, span], preferred_element_type=F32)
        part = jnp.where(inside, part, 0.0)
        for t in range(lo, hi):
            attn[t] = attn[t] + part[:, (t - lo) * LANES : (t - lo + 1) * LANES]
    attn = jnp.concatenate(attn, axis=1).astype(BF16)
    enc_x = jnp.concatenate([pick(3 * tiles + t, mine).astype(F32) for t in range(model // LANES)], axis=1)
    resid = enc_x + jnp.dot(attn, w_eo_ref[...], preferred_element_type=F32)
    center = resid - jnp.mean(resid, axis=-1, keepdims=True)
    spread = jnp.mean(center * center, axis=-1, keepdims=True)
    features = (center * lax.rsqrt(spread + 1e-05)).astype(BF16)
    out_ref[...] = jnp.dot(features, w_kv_ref[...], preferred_element_type=F32).astype(BF16)


def attend_kernel(count_ref, query_ref, cache_ref, new_ref, out_ref):
    filled = count_ref[0]
    slots, length, both = cache_ref.shape
    width = both // 2
    kv_heads = width // HD
    per = query_ref.shape[0] // kv_heads
    query = query_ref[...]
    scores = []
    for g in range(kv_heads):
        head = query[g * per : (g + 1) * per]
        cols = slice(g * HD, (g + 1) * HD)
        keys = cache_ref[:, :, cols].reshape(slots * length, HD)
        old = lax.dot_general(head, keys, (((1,), (1,)), ((), ())), preferred_element_type=F32)
        new = lax.dot_general(head, new_ref[:, cols], (((1,), (1,)), ((), ())), preferred_element_type=F32)
        scores.append(jnp.concatenate([old, new], axis=1))
    scores = jnp.concatenate(scores, axis=0) * HD ** (-0.5)
    slot = lax.broadcasted_iota(jnp.int32, scores.shape, 1) // length
    scores = jnp.where((slot < filled) | (slot == slots), scores, -jnp.inf)
    powers = jnp.exp(scores - jnp.max(scores, axis=-1, keepdims=True))
    weights = (powers / jnp.sum(powers, axis=-1, keepdims=True)).astype(BF16)
    copies = out_ref.shape[0]
    for g in range(kv_heads):
        mine = weights[g * per : (g + 1) * per]
        cols = slice(width + g * HD, width + (g + 1) * HD)
        values = cache_ref[:, :, cols].reshape(slots * length, HD)
        part = jnp.dot(mine[:, : slots * length], values, preferred_element_type=F32)
        part = part + jnp.dot(mine[:, slots * length :], new_ref[:, cols], preferred_element_type=F32)
        part = part.astype(BF16)
        halves = kv_heads // 2
        for copy in range(g // halves, copies, 2):
            out_ref[copy, g % halves] = part


def finish_kernel(attn_ref, dec_x_ref, out_ref):
    attn = attn_ref[...].astype(F32)
    for k in range(attn.shape[0]):
        cols = slice(k * LANES, (k + 1) * LANES)
        out_ref[:, cols] = (dec_x_ref[:, cols].astype(F32) + attn[k : k + 1]).astype(BF16)


def finish_sums_kernel(sums_ref, dec_x_ref, out_ref, rows_ref, attn_ref):
    attn_ref[...] = add_halves(sums_ref, rows_ref)
    finish_kernel(attn_ref, dec_x_ref, out_ref)


def solution(mesh):
    devices = mesh.shape["seq"]
    swap = [(i, i ^ 1) for i in range(devices)]

    def exchange(sent):
        return lax.all_to_all(sent, "seq", 0, 0, tiled=True)

    def project(copies, weight, mate, *ready):
        depth, cols = weight.shape
        lanes = min(cols, LANES)
        sums = pl.pallas_call(
            project_kernel,
            out_shape=jax.ShapeDtypeStruct((devices, 2, cols // lanes, lanes), F32),
            in_specs=[VMEM] * 3 + [ANY] * len(ready),
            out_specs=VMEM,
            scratch_shapes=[pltpu.VMEM((devices * SUB, LANES), F32), pltpu.VMEM((devices, depth // 2), BF16)],
            compiler_params=params(8),
            cost_estimate=LONG,
        )(copies, weight, mate, *ready)
        return exchange(sums)

    def add_up(sums):
        sums = sums.reshape(devices // 2, 2, -1)
        return (sums[:, 0] + sums[:, 1]).astype(BF16).reshape(-1, LANES)

    def local(enc_x, enc_qkv, w_eo, w_kv, dec_x, w_q, w_o, cache_kv, doc_tile, cached_count):
        qkv = enc_qkv.transpose(1, 0, 2)
        w_q_mate = lax.ppermute(w_q, "seq", swap)
        w_o_mate = lax.ppermute(w_o, "seq", swap)
        blocks = (enc_qkv.size + enc_x.size) // (SUB * LANES)
        share = blocks // (2 * SHARES)
        rest = blocks - 2 * SHARES * share
        groups = dec_x.size // (2 * SUB * LANES) + rest + share
        rows = pltpu.VMEM((dec_x.shape[1] // LANES, LANES), F32)
        packed = pl.pallas_call(
            pack_kernel,
            out_shape=jax.ShapeDtypeStruct((devices, groups, SUB, LANES), BF16),
            in_specs=[ANY] * 3,
            out_specs=VMEM,
            scratch_shapes=[
                pltpu.VMEM(dec_x.shape, BF16),
                pltpu.VMEM(qkv.shape, BF16),
                pltpu.VMEM(enc_x.shape, BF16),
                rows,
                pltpu.SemaphoreType.DMA((3,)),
            ],
            compiler_params=params(40),
            cost_estimate=LONG,
        )(dec_x, qkv, enc_x)
        copies = exchange(packed)
        mine = pl.pallas_call(
            share_kernel,
            out_shape=jax.ShapeDtypeStruct((devices, share, SUB, LANES), BF16),
            in_specs=[VMEM],
            out_specs=VMEM,
            compiler_params=params(1),
        )(copies)
        shares = [lax.ppermute(mine, "seq", [(i, i ^ (2 * j)) for i in range(devices)]) for j in range(1, SHARES)]
        sums = project(copies, w_q, w_q_mate, w_o_mate)
        if sums.shape[-1] == LANES:
            query = pl.pallas_call(
                collect_kernel,
                out_shape=jax.ShapeDtypeStruct((sums.size // (2 * LANES), LANES), BF16),
                in_specs=[VMEM],
                out_specs=VMEM,
                scratch_shapes=[rows],
                compiler_params=params(1),
            )(sums)
        else:
            query = add_up(sums)
        merged = pl.pallas_call(
            merge_kernel,
            out_shape=jax.ShapeDtypeStruct((SHARES * share, devices * SUB, LANES), BF16),
            in_specs=[VMEM] * 5,
            out_specs=VMEM,
            compiler_params=params(4),
            cost_estimate=LONG,
        )(query, mine, *shares)
        new_kv = pl.pallas_call(
            encode_kernel,
            out_shape=jax.ShapeDtypeStruct((TILE_LEN, w_kv.shape[1]), BF16),
            in_specs=[SMEM] + [VMEM] * 5,
            out_specs=VMEM,
            compiler_params=params(12),
            cost_estimate=LONG,
        )(doc_tile, copies, merged, lax.ppermute(merged, "seq", swap), w_eo, w_kv)
        heads = query.shape[0]
        copies = pl.pallas_call(
            attend_kernel,
            out_shape=jax.ShapeDtypeStruct((devices, heads // (2 * SUB), SUB, LANES), BF16),
            in_specs=[SMEM] + [VMEM] * 3,
            out_specs=VMEM,
            compiler_params=params(4),
            cost_estimate=LONG,
        )(cached_count, query, cache_kv[0], new_kv)
        sums = project(exchange(copies), w_o, w_o_mate)
        if sums.shape[-1] == LANES:
            kernel, scratch, attn = finish_sums_kernel, [rows, pltpu.VMEM((heads, LANES), BF16)], sums
        else:
            kernel, scratch, attn = finish_kernel, [], add_up(sums)
        return pl.pallas_call(
            kernel,
            out_shape=jax.ShapeDtypeStruct(dec_x.shape, BF16),
            in_specs=[VMEM] * 2,
            out_specs=VMEM,
            scratch_shapes=scratch,
            compiler_params=params(2),
            cost_estimate=LONG,
        )(attn, dec_x)

    return jax.shard_map(
        local,
        mesh=mesh,
        in_specs=(
            P(("group", "seq"), None),
            P(("group", "seq"), None, None),
            P(),
            P(),
            P(("group", "seq"), None),
            P(None, "seq"),
            P(None, "seq"),
            P(("group", "seq"), None, None, None),
            P(("group", "seq")),
            P(("group", "seq")),
        ),
        out_specs=P(("group", "seq"), None),
        check_vma=False,
    )
```

```python
import functools

import jax
import jax.numpy as jnp
from jax import lax
from jax.experimental import pallas as pl
from jax.experimental.pallas import tpu as pltpu
from jax.sharding import PartitionSpec as P

EH = 8
EHD = 80
HD = 128
TILE_LEN = 128
LANES = 128
SUB = 8
SHARES = 4
CHUNK = 512
VMEM = pl.BlockSpec(memory_space=pltpu.VMEM)
ANY = pl.BlockSpec(memory_space=pl.ANY)
SMEM = pl.BlockSpec(memory_space=pltpu.SMEM)
LONG = pl.CostEstimate(flops=10**10, transcendentals=0, bytes_accessed=10**7)
F32 = jnp.float32
BF16 = jnp.bfloat16


def params(mib):
    return pltpu.CompilerParams(vmem_limit_bytes=mib * 1024 * 1024)


def pack_kernel(width, rows_in_ref, out_ref, rows_ref):
    x = rows_in_ref[SUB : SUB + 1, :].astype(F32)
    scale = lax.rsqrt(jnp.mean(x * x, axis=-1, keepdims=True) + 1e-05)
    normed = x * scale
    groups = x.shape[1] // LANES
    for k in range(groups):
        rows_ref[k : k + 1, :] = normed[:, k * LANES : (k + 1) * LANES]
    copies = out_ref.shape[0]

    def put(place, block, to):
        block = block.astype(BF16)
        for copy in to:
            out_ref[copy, place] = block

    halves = groups // SUB // 2
    for i in range(2 * halves):
        put(i % halves, rows_ref[i * SUB : (i + 1) * SUB, :], range(i // halves, copies, 2))
    blocks = [rows_in_ref[:SUB, t : t + LANES] for t in range(0, width, LANES)]
    share = len(blocks) // (2 * SHARES)
    for i, block in enumerate(blocks[2 * SHARES * share :]):
        put(halves + i, block, range(copies))
    first = out_ref.shape[1] - share
    for i, block in enumerate(blocks[: 2 * SHARES * share]):
        core, chip = divmod(i // share, SHARES)
        put(first + i % share, block, range(2 * chip + core, copies, 2 * SHARES))


def project_kernel(sent_ref, w_ref, mate_ref, *refs):
    out_ref, rows_ref, x_ref = refs[-3:]
    docs, half = x_ref.shape
    for i in range(half // (SUB * LANES)):
        rows_ref[...] = sent_ref[:, i].astype(F32).reshape(docs * SUB, LANES)
        for j in range(SUB):
            k = i * SUB + j
            x_ref[:, k * LANES : (k + 1) * LANES] = rows_ref[pl.ds(j, docs, stride=SUB), :].astype(BF16)
    core = lax.rem(lax.axis_index("seq"), 2)
    parts, lanes = out_ref.shape[2:]

    def multiply(side):
        for ref, place in ((w_ref, side), (mate_ref, 1 - side)):
            result = jnp.zeros((docs, ref.shape[1]), F32)
            for k in range(0, half, CHUNK):
                rows = slice(side * half + k, side * half + k + CHUNK)
                result += jnp.dot(x_ref[:, k : k + CHUNK], ref[rows, :], preferred_element_type=F32)
            result = jnp.stack([result[:, p * lanes : (p + 1) * lanes] for p in range(parts)], axis=1)
            out_ref[:, place] = result

    for side in range(2):
        pl.when(core == side)(functools.partial(multiply, side))


def add_halves(sums_ref, rows_ref):
    devices, cores, parts, _ = sums_ref.shape
    for chip in range(devices // 2):
        for core in range(cores):
            row = (chip * cores + core) * parts
            rows_ref[row : row + parts, :] = sums_ref[2 * chip, core] + sums_ref[2 * chip + 1, core]
    return rows_ref[...].astype(BF16)


def collect_kernel(sums_ref, out_ref, rows_ref):
    out_ref[...] = add_halves(sums_ref, rows_ref)


def share_kernel(own_ref, out_ref):
    share = out_ref.shape[1]
    out_ref[...] = own_ref[:, own_ref.shape[1] - share :]


def merge(block):
    return block.astype(F32).reshape(-1, LANES).astype(BF16)


def merge_kernel(query_ref, own_0, own_1, own_2, own_3, out_ref):
    share = own_0.shape[1]
    place = lax.rem(lax.axis_index("seq") // 2, SHARES)
    for j, ref in enumerate((own_0, own_1, own_2, own_3)):
        start = jnp.bitwise_xor(place, j) * share
        for i in range(share):
            out_ref[start + i] = merge(ref[:, i])


def encode_kernel(tile_ref, sent_ref, own_ref, other_ref, w_eo_ref, w_kv_ref, out_ref):
    width, model = w_eo_ref.shape
    tiles = width // LANES
    held = own_ref.shape[0]
    rest = 3 * tiles + model // LANES - 2 * held
    first = sent_ref.shape[1] - held // SHARES - rest
    core = lax.rem(lax.axis_index("seq"), 2)
    mine = pl.ds(pl.multiple_of(tile_ref[0] * TILE_LEN, TILE_LEN), TILE_LEN)

    def pick(place, rows):
        if place >= 2 * held:
            chunk = TILE_LEN // SUB
            block = sent_ref[pl.ds(tile_ref[0] * chunk, chunk), first + place - 2 * held]
            return merge(block)
        side, index = divmod(place, held)
        return jnp.where(core == side, own_ref[index, rows], other_ref[index, rows])

    every = slice(None)
    query = jnp.concatenate([pick(t, mine) for t in range(tiles)], axis=1)
    keys = jnp.concatenate([pick(tiles + t, every) for t in range(tiles)], axis=1)
    values = jnp.concatenate([pick(2 * tiles + t, every) for t in range(tiles)], axis=1)
    column = lax.broadcasted_iota(jnp.int32, (TILE_LEN, width), 1)
    spans, insides, scores, weights = [], [], [], []
    for h in range(EH):
        span = slice(h * EHD // LANES * LANES, ((h + 1) * EHD - 1) // LANES * LANES + LANES)
        inside = (column[:, span] >= h * EHD) & (column[:, span] < (h + 1) * EHD)
        head = jnp.where(inside, query[:, span], jnp.zeros((), BF16))
        score = lax.dot_general(head, keys[:, span], (((1,), (1,)), ((), ())), preferred_element_type=F32)
        spans.append(span)
        insides.append(inside)
        scores.append(score * EHD ** (-0.5))
    for score in scores:
        powers = jnp.exp(score - jnp.max(score, axis=-1, keepdims=True))
        weights.append((powers / jnp.sum(powers, axis=-1, keepdims=True)).astype(BF16))
    attn = [jnp.zeros((TILE_LEN, LANES), F32) for _ in range(tiles)]
    for span, inside, weight in zip(spans, insides, weights):
        part = jnp.where(inside, jnp.dot(weight, values[:, span], preferred_element_type=F32), 0.0)
        for t in range(span.start // LANES, span.stop // LANES):
            start = t * LANES - span.start
            attn[t] = attn[t] + part[:, start : start + LANES]
    attn = jnp.concatenate(attn, axis=1).astype(BF16)
    enc_x = jnp.concatenate([pick(3 * tiles + t, mine).astype(F32) for t in range(model // LANES)], axis=1)
    resid = enc_x + jnp.dot(attn, w_eo_ref[...], preferred_element_type=F32)
    center = resid - jnp.mean(resid, axis=-1, keepdims=True)
    spread = jnp.mean(center * center, axis=-1, keepdims=True)
    features = (center * lax.rsqrt(spread + 1e-05)).astype(BF16)
    out_ref[...] = jnp.dot(features, w_kv_ref[...], preferred_element_type=F32).astype(BF16)


def attend_kernel(count_ref, query_ref, cache_ref, new_ref, out_ref):
    filled = count_ref[0]
    slots, length, both = cache_ref.shape
    width = both // 2
    kv_heads = width // HD
    per = query_ref.shape[0] // kv_heads
    query = query_ref[...]
    scores = []
    for g in range(kv_heads):
        head = query[g * per : (g + 1) * per]
        cols = slice(g * HD, (g + 1) * HD)
        keys = cache_ref[:, :, cols].reshape(slots * length, HD)
        old = lax.dot_general(head, keys, (((1,), (1,)), ((), ())), preferred_element_type=F32)
        new = lax.dot_general(head, new_ref[:, cols], (((1,), (1,)), ((), ())), preferred_element_type=F32)
        scores.append(jnp.concatenate([old, new], axis=1))
    scores = jnp.concatenate(scores, axis=0) * HD ** (-0.5)
    slot = lax.broadcasted_iota(jnp.int32, scores.shape, 1) // length
    scores = jnp.where((slot < filled) | (slot == slots), scores, -jnp.inf)
    powers = jnp.exp(scores - jnp.max(scores, axis=-1, keepdims=True))
    weights = (powers / jnp.sum(powers, axis=-1, keepdims=True)).astype(BF16)
    copies = out_ref.shape[0]
    for g in range(kv_heads):
        mine = weights[g * per : (g + 1) * per]
        cols = slice(width + g * HD, width + (g + 1) * HD)
        values = cache_ref[:, :, cols].reshape(slots * length, HD)
        part = jnp.dot(mine[:, : slots * length], values, preferred_element_type=F32)
        part = part + jnp.dot(mine[:, slots * length :], new_ref[:, cols], preferred_element_type=F32)
        part = part.astype(BF16)
        halves = kv_heads // 2
        for copy in range(g // halves, copies, 2):
            out_ref[copy, g % halves] = part


def finish_kernel(attn_ref, dec_x_ref, out_ref):
    attn = attn_ref[...].astype(F32)
    for k in range(attn.shape[0]):
        cols = slice(k * LANES, (k + 1) * LANES)
        out_ref[:, cols] = (dec_x_ref[:, cols].astype(F32) + attn[k : k + 1]).astype(BF16)


def finish_sums_kernel(sums_ref, dec_x_ref, out_ref, rows_ref, attn_ref):
    attn_ref[...] = add_halves(sums_ref, rows_ref)
    finish_kernel(attn_ref, dec_x_ref, out_ref)


def solution(mesh):
    devices = mesh.shape["seq"]
    swap = [(i, i ^ 1) for i in range(devices)]

    def exchange(sent):
        return lax.all_to_all(sent, "seq", 0, 0, tiled=True)

    def project(copies, weight, mate, *ready):
        depth, cols = weight.shape
        lanes = min(cols, LANES)
        sums = pl.pallas_call(
            project_kernel,
            out_shape=jax.ShapeDtypeStruct((devices, 2, cols // lanes, lanes), F32),
            in_specs=[VMEM] * 3 + [ANY] * len(ready),
            out_specs=VMEM,
            scratch_shapes=[pltpu.VMEM((devices * SUB, LANES), F32), pltpu.VMEM((devices, depth // 2), BF16)],
            compiler_params=params(8),
            cost_estimate=LONG,
        )(copies, weight, mate, *ready)
        return exchange(sums)

    def add_up(sums):
        sums = sums.reshape(devices // 2, 2, -1)
        return (sums[:, 0] + sums[:, 1]).astype(BF16).reshape(-1, LANES)

    def local(enc_x, enc_qkv, w_eo, w_kv, dec_x, w_q, w_o, cache_kv, doc_tile, cached_count):
        width = (enc_qkv.size + enc_x.size) // SUB
        spare = jnp.zeros((SUB, dec_x.shape[1] - width), BF16)
        rows_in = jnp.concatenate([enc_qkv.reshape(SUB, -1), enc_x, spare], axis=1)
        rows_in = jnp.concatenate([rows_in, dec_x], axis=0)
        w_q_mate = lax.ppermute(w_q, "seq", swap)
        w_o_mate = lax.ppermute(w_o, "seq", swap)
        blocks = (enc_qkv.size + enc_x.size) // (SUB * LANES)
        share = blocks // (2 * SHARES)
        rest = blocks - 2 * SHARES * share
        groups = dec_x.size // (2 * SUB * LANES) + rest + share
        rows = pltpu.VMEM((dec_x.shape[1] // LANES, LANES), F32)
        packed = pl.pallas_call(
            functools.partial(pack_kernel, width),
            out_shape=jax.ShapeDtypeStruct((devices, groups, SUB, LANES), BF16),
            in_specs=[VMEM],
            out_specs=VMEM,
            scratch_shapes=[rows],
            compiler_params=params(2),
            cost_estimate=LONG,
        )(rows_in)
        copies = exchange(packed)
        mine = pl.pallas_call(
            share_kernel,
            out_shape=jax.ShapeDtypeStruct((devices, share, SUB, LANES), BF16),
            in_specs=[VMEM],
            out_specs=VMEM,
            compiler_params=params(1),
        )(copies)
        shares = [lax.ppermute(mine, "seq", [(i, i ^ (2 * j)) for i in range(devices)]) for j in range(1, SHARES)]
        sums = project(copies, w_q, w_q_mate, w_o_mate)
        if sums.shape[-1] == LANES:
            query = pl.pallas_call(
                collect_kernel,
                out_shape=jax.ShapeDtypeStruct((sums.size // (2 * LANES), LANES), BF16),
                in_specs=[VMEM],
                out_specs=VMEM,
                scratch_shapes=[rows],
                compiler_params=params(1),
            )(sums)
        else:
            query = add_up(sums)
        merged = pl.pallas_call(
            merge_kernel,
            out_shape=jax.ShapeDtypeStruct((SHARES * share, devices * SUB, LANES), BF16),
            in_specs=[VMEM] * 5,
            out_specs=VMEM,
            compiler_params=params(4),
            cost_estimate=LONG,
        )(query, mine, *shares)
        new_kv = pl.pallas_call(
            encode_kernel,
            out_shape=jax.ShapeDtypeStruct((TILE_LEN, w_kv.shape[1]), BF16),
            in_specs=[SMEM] + [VMEM] * 5,
            out_specs=VMEM,
            compiler_params=params(12),
            cost_estimate=LONG,
        )(doc_tile, copies, merged, lax.ppermute(merged, "seq", swap), w_eo, w_kv)
        heads = query.shape[0]
        copies = pl.pallas_call(
            attend_kernel,
            out_shape=jax.ShapeDtypeStruct((devices, heads // (2 * SUB), SUB, LANES), BF16),
            in_specs=[SMEM] + [VMEM] * 3,
            out_specs=VMEM,
            compiler_params=params(4),
            cost_estimate=LONG,
        )(cached_count, query, cache_kv[0], new_kv)
        sums = project(exchange(copies), w_o, w_o_mate)
        if sums.shape[-1] == LANES:
            kernel, scratch, attn = finish_sums_kernel, [rows, pltpu.VMEM((heads, LANES), BF16)], sums
        else:
            kernel, scratch, attn = finish_kernel, [], add_up(sums)
        return pl.pallas_call(
            kernel,
            out_shape=jax.ShapeDtypeStruct(dec_x.shape, BF16),
            in_specs=[VMEM] * 2,
            out_specs=VMEM,
            scratch_shapes=scratch,
            compiler_params=params(2),
            cost_estimate=LONG,
        )(attn, dec_x)

    return jax.shard_map(
        local,
        mesh=mesh,
        in_specs=(
            P(("group", "seq"), None),
            P(("group", "seq"), None, None),
            P(),
            P(),
            P(("group", "seq"), None),
            P(None, "seq"),
            P(None, "seq"),
            P(("group", "seq"), None, None, None),
            P(("group", "seq")),
            P(("group", "seq")),
        ),
        out_specs=P(("group", "seq"), None),
        check_vma=False,
    )
```

```python
import functools

import jax
import jax.numpy as jnp
from jax import lax
from jax.experimental import pallas as pl
from jax.experimental.pallas import tpu as pltpu
from jax.sharding import PartitionSpec as P

EH = 8
EHD = 80
HD = 128
TILE_LEN = 128
LANES = 128
SUB = 8
SHARES = 4
EARLY = 2
CHUNK = 512
VMEM = pl.BlockSpec(memory_space=pltpu.VMEM)
SMEM = pl.BlockSpec(memory_space=pltpu.SMEM)
ANY = pl.BlockSpec(memory_space=pl.ANY)
LONG = pl.CostEstimate(flops=10**10, transcendentals=0, bytes_accessed=10**7)
F32 = jnp.float32
BF16 = jnp.bfloat16


def params(mib):
    return pltpu.CompilerParams(vmem_limit_bytes=mib * 1024 * 1024)


def pack_kernel(width, rows_in_ref, out_ref, rows_ref):
    x = rows_in_ref[SUB : SUB + 1, :].astype(F32)
    scale = lax.rsqrt(jnp.mean(x * x, axis=-1, keepdims=True) + 1e-05)
    normed = x * scale
    groups = x.shape[1] // LANES
    for k in range(groups):
        rows_ref[k : k + 1, :] = normed[:, k * LANES : (k + 1) * LANES]
    copies = out_ref.shape[0]

    def put(place, block, to):
        block = block.astype(BF16)
        for copy in to:
            out_ref[copy, place] = block

    halves = groups // SUB // 2
    for i in range(2 * halves):
        put(i % halves, rows_ref[i * SUB : (i + 1) * SUB, :], range(i // halves, copies, 2))
    blocks = [rows_in_ref[:SUB, t : t + LANES] for t in range(0, width, LANES)]
    share = len(blocks) // (2 * SHARES)
    for i, block in enumerate(blocks[2 * SHARES * share :]):
        put(halves + i, block, range(copies))
    first = out_ref.shape[1] - share
    for i, block in enumerate(blocks[: 2 * SHARES * share]):
        early = i < 2 * SHARES * EARLY
        each = EARLY if early else share - EARLY
        piece, place = divmod(i if early else i - 2 * SHARES * EARLY, each)
        core, chip = divmod(piece, SHARES)
        place += first if early else first + EARLY
        put(place, block, range(2 * chip + core, copies, 2 * SHARES))


def project_kernel(sent_ref, w_ref, mate_ref, *refs):
    out_ref, rows_ref, x_ref = refs[-3:]
    docs, half = x_ref.shape
    for i in range(half // (SUB * LANES)):
        rows_ref[...] = sent_ref[:, i].astype(F32).reshape(docs * SUB, LANES)
        for j in range(SUB):
            k = i * SUB + j
            x_ref[:, k * LANES : (k + 1) * LANES] = rows_ref[pl.ds(j, docs, stride=SUB), :].astype(BF16)
    core = lax.rem(lax.axis_index("seq"), 2)
    parts, lanes = out_ref.shape[2:]

    def multiply(side):
        for ref, place in ((w_ref, side), (mate_ref, 1 - side)):
            result = jnp.zeros((docs, ref.shape[1]), F32)
            for k in range(0, half, CHUNK):
                rows = slice(side * half + k, side * half + k + CHUNK)
                result += jnp.dot(x_ref[:, k : k + CHUNK], ref[rows, :], preferred_element_type=F32)
            result = jnp.stack([result[:, p * lanes : (p + 1) * lanes] for p in range(parts)], axis=1)
            out_ref[:, place] = result

    for side in range(2):
        pl.when(core == side)(functools.partial(multiply, side))


def add_halves(sums_ref, rows_ref):
    devices, cores, parts, _ = sums_ref.shape
    for chip in range(devices // 2):
        for core in range(cores):
            row = (chip * cores + core) * parts
            rows_ref[row : row + parts, :] = sums_ref[2 * chip, core] + sums_ref[2 * chip + 1, core]
    return rows_ref[...].astype(BF16)


def collect_kernel(sums_ref, out_ref, rows_ref):
    out_ref[...] = add_halves(sums_ref, rows_ref)


def share_kernel(own_ref, out_ref):
    share = out_ref.shape[1]
    out_ref[...] = own_ref[:, own_ref.shape[1] - share :]


def merge(block):
    return block.astype(F32).reshape(-1, LANES).astype(BF16)


def merge_kernel(start, query_ref, own_0, own_1, own_2, own_3, out_ref):
    share = out_ref.shape[0] // SHARES
    place = lax.rem(lax.axis_index("seq") // 2, SHARES)
    for j, ref in enumerate((own_0, own_1, own_2, own_3)):
        for i in range(share):
            out_ref[jnp.bitwise_xor(place, j) * share + i] = merge(ref[:, start + i])


def pick(place, rows, own_ref, other_ref):
    held = own_ref.shape[0]
    core = lax.rem(lax.axis_index("seq"), 2)
    side, index = divmod(place, held)
    return jnp.where(core == side, own_ref[index, rows], other_ref[index, rows])


def rows_of(tile_ref):
    return pl.ds(pl.multiple_of(tile_ref[0] * TILE_LEN, TILE_LEN), TILE_LEN)


def attention_kernel(tile_ref, own_ref, other_ref, out_ref):
    width = out_ref.shape[1]
    tiles = width // LANES
    mine = rows_of(tile_ref)
    every = slice(None)
    query = jnp.concatenate([pick(t, mine, own_ref, other_ref) for t in range(tiles)], axis=1)
    keys = jnp.concatenate([pick(tiles + t, every, own_ref, other_ref) for t in range(tiles)], axis=1)
    values = jnp.concatenate([pick(2 * tiles + t, every, own_ref, other_ref) for t in range(tiles)], axis=1)
    column = lax.broadcasted_iota(jnp.int32, (TILE_LEN, width), 1)
    spans, insides, scores, weights = [], [], [], []
    for h in range(EH):
        span = slice(h * EHD // LANES * LANES, ((h + 1) * EHD - 1) // LANES * LANES + LANES)
        inside = (column[:, span] >= h * EHD) & (column[:, span] < (h + 1) * EHD)
        head = jnp.where(inside, query[:, span], jnp.zeros((), BF16))
        score = lax.dot_general(head, keys[:, span], (((1,), (1,)), ((), ())), preferred_element_type=F32)
        spans.append(span)
        insides.append(inside)
        scores.append(score * EHD ** (-0.5))
    for score in scores:
        powers = jnp.exp(score - jnp.max(score, axis=-1, keepdims=True))
        weights.append((powers / jnp.sum(powers, axis=-1, keepdims=True)).astype(BF16))
    attn = [jnp.zeros((TILE_LEN, LANES), F32) for _ in range(tiles)]
    for span, inside, weight in zip(spans, insides, weights):
        part = jnp.where(inside, jnp.dot(weight, values[:, span], preferred_element_type=F32), 0.0)
        for t in range(span.start // LANES, span.stop // LANES):
            start = t * LANES - span.start
            attn[t] = attn[t] + part[:, start : start + LANES]
    out_ref[...] = jnp.concatenate(attn, axis=1).astype(BF16)


def features_kernel(
    tile_ref, attn_ref, sent_ref, own_ref, other_ref, own_late, other_late, w_eo_ref, w_kv_ref, out_ref
):
    width, model = w_eo_ref.shape
    mine = rows_of(tile_ref)
    early, late = 2 * own_ref.shape[0], 2 * own_late.shape[0]
    first = 3 * width // LANES
    enc_x = [pick(t, mine, own_ref, other_ref) for t in range(first, early)]
    enc_x += [pick(t, mine, own_late, other_late) for t in range(late)]
    chunk = TILE_LEN // SUB
    rest = first + model // LANES - early - late
    last = sent_ref.shape[1] - (early + late) // (2 * SHARES)
    enc_x += [merge(sent_ref[pl.ds(tile_ref[0] * chunk, chunk), t]) for t in range(last - rest, last)]
    enc_x = jnp.concatenate(enc_x, axis=1).astype(F32)
    resid = enc_x + jnp.dot(attn_ref[...], w_eo_ref[...], preferred_element_type=F32)
    center = resid - jnp.mean(resid, axis=-1, keepdims=True)
    spread = jnp.mean(center * center, axis=-1, keepdims=True)
    features = (center * lax.rsqrt(spread + 1e-05)).astype(BF16)
    out_ref[...] = jnp.dot(features, w_kv_ref[...], preferred_element_type=F32).astype(BF16)


def scores_kernel(query_ref, keys_ref, _, out_ref):
    slots, length, width = keys_ref.shape[0], keys_ref.shape[1], keys_ref.shape[2] // 2
    kv_heads = width // HD
    per = query_ref.shape[0] // kv_heads
    for g in range(kv_heads):
        keys = keys_ref[:, :, g * HD : (g + 1) * HD].reshape(slots * length, HD)
        rows = slice(g * per, (g + 1) * per)
        out_ref[rows, :] = lax.dot_general(
            query_ref[rows, :], keys, (((1,), (1,)), ((), ())), preferred_element_type=F32
        ) * HD ** (-0.5)


def attend_kernel(count_ref, query_ref, scores_ref, cache_ref, new_ref, out_ref):
    slots, length, both = cache_ref.shape
    width = both // 2
    kv_heads = width // HD
    per = query_ref.shape[0] // kv_heads
    scores = []
    for g in range(kv_heads):
        keys = new_ref[:, g * HD : (g + 1) * HD]
        head = query_ref[g * per : (g + 1) * per, :]
        scores.append(lax.dot_general(head, keys, (((1,), (1,)), ((), ())), preferred_element_type=F32))
    scores = jnp.concatenate(scores, axis=0) * HD ** (-0.5)
    slot = lax.broadcasted_iota(jnp.int32, scores_ref.shape, 1) // length
    old = jnp.where(slot < count_ref[0], scores_ref[...], -jnp.inf)
    scores = jnp.concatenate([old, scores], axis=1)
    powers = jnp.exp(scores - jnp.max(scores, axis=-1, keepdims=True))
    weights = (powers / jnp.sum(powers, axis=-1, keepdims=True)).astype(BF16)
    copies = out_ref.shape[0]
    for g in range(kv_heads):
        mine = weights[g * per : (g + 1) * per]
        cols = slice(width + g * HD, width + (g + 1) * HD)
        values = cache_ref[:, :, cols].reshape(slots * length, HD)
        part = jnp.dot(mine[:, : slots * length], values, preferred_element_type=F32)
        part = part + jnp.dot(mine[:, slots * length :], new_ref[:, cols], preferred_element_type=F32)
        part = part.astype(BF16)
        halves = kv_heads // 2
        for copy in range(g // halves, copies, 2):
            out_ref[copy, g % halves] = part


def finish_kernel(attn_ref, dec_x_ref, out_ref):
    attn = attn_ref[...].astype(F32)
    for k in range(attn.shape[0]):
        cols = slice(k * LANES, (k + 1) * LANES)
        out_ref[:, cols] = (dec_x_ref[:, cols].astype(F32) + attn[k : k + 1]).astype(BF16)


def finish_sums_kernel(sums_ref, dec_x_ref, out_ref, rows_ref, attn_ref):
    attn_ref[...] = add_halves(sums_ref, rows_ref)
    finish_kernel(attn_ref, dec_x_ref, out_ref)


def solution(mesh):
    devices = mesh.shape["seq"]
    swap = [(i, i ^ 1) for i in range(devices)]

    def exchange(sent):
        return lax.all_to_all(sent, "seq", 0, 0, tiled=True)

    def project(copies, weight, mate, *ready):
        depth, cols = weight.shape
        lanes = min(cols, LANES)
        sums = pl.pallas_call(
            project_kernel,
            out_shape=jax.ShapeDtypeStruct((devices, 2, cols // lanes, lanes), F32),
            in_specs=[VMEM] * 3 + [ANY] * len(ready),
            out_specs=VMEM,
            scratch_shapes=[pltpu.VMEM((devices * SUB, LANES), F32), pltpu.VMEM((devices, depth // 2), BF16)],
            compiler_params=params(8),
            cost_estimate=LONG,
        )(copies, weight, mate, *ready)
        return exchange(sums)

    def add_up(sums):
        sums = sums.reshape(devices // 2, 2, -1)
        return (sums[:, 0] + sums[:, 1]).astype(BF16).reshape(-1, LANES)

    def local(enc_x, enc_qkv, w_eo, w_kv, dec_x, w_q, w_o, cache_kv, doc_tile, cached_count):
        width = (enc_qkv.size + enc_x.size) // SUB
        spare = jnp.zeros((SUB, dec_x.shape[1] - width), BF16)
        rows_in = jnp.concatenate([enc_qkv.reshape(SUB, -1), enc_x, spare], axis=1)
        rows_in = jnp.concatenate([rows_in, dec_x], axis=0)
        w_q_mate = lax.ppermute(w_q, "seq", swap)
        w_o_mate = lax.ppermute(w_o, "seq", swap)
        blocks = (enc_qkv.size + enc_x.size) // (SUB * LANES)
        share = blocks // (2 * SHARES)
        rest = blocks - 2 * SHARES * share
        groups = dec_x.size // (2 * SUB * LANES) + rest + share
        rows = pltpu.VMEM((dec_x.shape[1] // LANES, LANES), F32)
        packed = pl.pallas_call(
            functools.partial(pack_kernel, width),
            out_shape=jax.ShapeDtypeStruct((devices, groups, SUB, LANES), BF16),
            in_specs=[VMEM],
            out_specs=VMEM,
            scratch_shapes=[rows],
            compiler_params=params(2),
            cost_estimate=LONG,
        )(rows_in)
        copies = exchange(packed)
        mine = pl.pallas_call(
            share_kernel,
            out_shape=jax.ShapeDtypeStruct((devices, share, SUB, LANES), BF16),
            in_specs=[VMEM],
            out_specs=VMEM,
            compiler_params=params(1),
        )(copies)
        shares = [lax.ppermute(mine, "seq", [(i, i ^ (2 * j)) for i in range(devices)]) for j in range(1, SHARES)]
        sums = project(copies, w_q, w_q_mate, w_o_mate)
        if sums.shape[-1] == LANES:
            query = pl.pallas_call(
                collect_kernel,
                out_shape=jax.ShapeDtypeStruct((sums.size // (2 * LANES), LANES), BF16),
                in_specs=[VMEM],
                out_specs=VMEM,
                scratch_shapes=[rows],
                compiler_params=params(1),
            )(sums)
        else:
            query = add_up(sums)
        def merge_part(start, count):
            merged = pl.pallas_call(
                functools.partial(merge_kernel, start),
                out_shape=jax.ShapeDtypeStruct((SHARES * count, devices * SUB, LANES), BF16),
                in_specs=[VMEM] * 5,
                out_specs=VMEM,
                compiler_params=params(4),
            )(query, mine, *shares)
            return merged, lax.ppermute(merged, "seq", swap)

        early = merge_part(0, EARLY)
        late = merge_part(EARLY, share - EARLY)
        cache = cache_kv[0]
        scores = pl.pallas_call(
            scores_kernel,
            out_shape=jax.ShapeDtypeStruct((query.shape[0], cache.shape[0] * TILE_LEN), F32),
            in_specs=[VMEM] * 2 + [ANY],
            out_specs=VMEM,
            compiler_params=params(4),
        )(query, cache, early[0])
        attn = pl.pallas_call(
            attention_kernel,
            out_shape=jax.ShapeDtypeStruct((TILE_LEN, w_eo.shape[0]), BF16),
            in_specs=[SMEM] + [VMEM] * 2,
            out_specs=VMEM,
            compiler_params=params(8),
        )(doc_tile, *early)
        new_kv = pl.pallas_call(
            features_kernel,
            out_shape=jax.ShapeDtypeStruct((TILE_LEN, w_kv.shape[1]), BF16),
            in_specs=[SMEM] + [VMEM] * 8,
            out_specs=VMEM,
            compiler_params=params(8),
            cost_estimate=LONG,
        )(doc_tile, attn, copies, *early, *late, w_eo, w_kv)
        heads = query.shape[0]
        copies = pl.pallas_call(
            attend_kernel,
            out_shape=jax.ShapeDtypeStruct((devices, heads // (2 * SUB), SUB, LANES), BF16),
            in_specs=[SMEM] + [VMEM] * 4,
            out_specs=VMEM,
            compiler_params=params(4),
            cost_estimate=LONG,
        )(cached_count, query, scores, cache, new_kv)
        sums = project(exchange(copies), w_o, w_o_mate)
        if sums.shape[-1] == LANES:
            kernel, scratch, attn = finish_sums_kernel, [rows, pltpu.VMEM((heads, LANES), BF16)], sums
        else:
            kernel, scratch, attn = finish_kernel, [], add_up(sums)
        return pl.pallas_call(
            kernel,
            out_shape=jax.ShapeDtypeStruct(dec_x.shape, BF16),
            in_specs=[VMEM] * 2,
            out_specs=VMEM,
            scratch_shapes=scratch,
            compiler_params=params(2),
            cost_estimate=LONG,
        )(attn, dec_x)

    return jax.shard_map(
        local,
        mesh=mesh,
        in_specs=(
            P(("group", "seq"), None),
            P(("group", "seq"), None, None),
            P(),
            P(),
            P(("group", "seq"), None),
            P(None, "seq"),
            P(None, "seq"),
            P(("group", "seq"), None, None, None),
            P(("group", "seq")),
            P(("group", "seq")),
        ),
        out_specs=P(("group", "seq"), None),
        check_vma=False,
    )
```

```python
import functools

import jax
import jax.numpy as jnp
from jax import lax
from jax.experimental import pallas as pl
from jax.experimental.pallas import tpu as pltpu
from jax.sharding import PartitionSpec as P

EH = 8
EHD = 80
HD = 128
TILE_LEN = 128
LANES = 128
SUB = 8
SHARES = 4
CHUNK = 512
VMEM = pl.BlockSpec(memory_space=pltpu.VMEM)
SMEM = pl.BlockSpec(memory_space=pltpu.SMEM)
ANY = pl.BlockSpec(memory_space=pl.ANY)
LONG = pl.CostEstimate(flops=10**10, transcendentals=0, bytes_accessed=10**7)
F32 = jnp.float32
BF16 = jnp.bfloat16


def params(mib):
    return pltpu.CompilerParams(vmem_limit_bytes=mib * 1024 * 1024)


def pack_kernel(width, rows_in_ref, out_ref, rows_ref):
    x = rows_in_ref[SUB : SUB + 1, :].astype(F32)
    scale = lax.rsqrt(jnp.mean(x * x, axis=-1, keepdims=True) + 1e-05)
    normed = x * scale
    groups = x.shape[1] // LANES
    for k in range(groups):
        rows_ref[k : k + 1, :] = normed[:, k * LANES : (k + 1) * LANES]
    copies = out_ref.shape[0]

    def put(place, block, to):
        block = block.astype(BF16)
        for copy in to:
            out_ref[copy, place] = block

    halves = groups // SUB // 2
    for i in range(2 * halves):
        put(i % halves, rows_ref[i * SUB : (i + 1) * SUB, :], range(i // halves, copies, 2))
    blocks = [rows_in_ref[:SUB, t : t + LANES] for t in range(0, width, LANES)]
    share = len(blocks) // (2 * SHARES)
    for i, block in enumerate(blocks[2 * SHARES * share :]):
        put(halves + i, block, range(copies))
    first = out_ref.shape[1] - share
    for i, block in enumerate(blocks[: 2 * SHARES * share]):
        core, chip = divmod(i // share, SHARES)
        put(first + i % share, block, range(2 * chip + core, copies, 2 * SHARES))


def project_kernel(sent_ref, w_ref, mate_ref, *refs):
    out_ref, rows_ref, x_ref = refs[-3:]
    docs, half = x_ref.shape
    for i in range(half // (SUB * LANES)):
        rows_ref[...] = sent_ref[:, i].astype(F32).reshape(docs * SUB, LANES)
        for j in range(SUB):
            k = i * SUB + j
            x_ref[:, k * LANES : (k + 1) * LANES] = rows_ref[pl.ds(j, docs, stride=SUB), :].astype(BF16)
    core = lax.rem(lax.axis_index("seq"), 2)
    parts, lanes = out_ref.shape[2:]

    def multiply(side):
        for ref, place in ((w_ref, side), (mate_ref, 1 - side)):
            result = jnp.zeros((docs, ref.shape[1]), F32)
            for k in range(0, half, CHUNK):
                rows = slice(side * half + k, side * half + k + CHUNK)
                result += jnp.dot(x_ref[:, k : k + CHUNK], ref[rows, :], preferred_element_type=F32)
            result = jnp.stack([result[:, p * lanes : (p + 1) * lanes] for p in range(parts)], axis=1)
            out_ref[:, place] = result

    for side in range(2):
        pl.when(core == side)(functools.partial(multiply, side))


def add_halves(sums_ref, rows_ref):
    devices, cores, parts, _ = sums_ref.shape
    for chip in range(devices // 2):
        for core in range(cores):
            row = (chip * cores + core) * parts
            rows_ref[row : row + parts, :] = sums_ref[2 * chip, core] + sums_ref[2 * chip + 1, core]
    return rows_ref[...].astype(BF16)


def collect_kernel(sums_ref, out_ref, rows_ref):
    out_ref[...] = add_halves(sums_ref, rows_ref)


def share_kernel(own_ref, out_ref):
    share = out_ref.shape[1]
    out_ref[...] = own_ref[:, own_ref.shape[1] - share :]


def merge(block):
    return block.astype(F32).reshape(-1, LANES).astype(BF16)


def merge_kernel(query_ref, own_0, own_1, own_2, own_3, out_ref):
    share = out_ref.shape[0] // SHARES
    place = lax.rem(lax.axis_index("seq") // 2, SHARES)
    for j, ref in enumerate((own_0, own_1, own_2, own_3)):
        for i in range(share):
            out_ref[jnp.bitwise_xor(place, j) * share + i] = merge(ref[:, i])


def pick(place, rows, own_ref, other_ref):
    held = own_ref.shape[0]
    core = lax.rem(lax.axis_index("seq"), 2)
    side, index = divmod(place, held)
    return jnp.where(core == side, own_ref[index, rows], other_ref[index, rows])


def rows_of(tile_ref):
    return pl.ds(pl.multiple_of(tile_ref[0] * TILE_LEN, TILE_LEN), TILE_LEN)


def attention_of(tile_ref, own_ref, other_ref, width):
    tiles = width // LANES
    mine = rows_of(tile_ref)
    every = slice(None)
    query = jnp.concatenate([pick(t, mine, own_ref, other_ref) for t in range(tiles)], axis=1)
    keys = jnp.concatenate([pick(tiles + t, every, own_ref, other_ref) for t in range(tiles)], axis=1)
    values = jnp.concatenate([pick(2 * tiles + t, every, own_ref, other_ref) for t in range(tiles)], axis=1)
    column = lax.broadcasted_iota(jnp.int32, (TILE_LEN, width), 1)
    spans, insides, scores, weights = [], [], [], []
    for h in range(EH):
        span = slice(h * EHD // LANES * LANES, ((h + 1) * EHD - 1) // LANES * LANES + LANES)
        inside = (column[:, span] >= h * EHD) & (column[:, span] < (h + 1) * EHD)
        head = jnp.where(inside, query[:, span], jnp.zeros((), BF16))
        score = lax.dot_general(head, keys[:, span], (((1,), (1,)), ((), ())), preferred_element_type=F32)
        spans.append(span)
        insides.append(inside)
        scores.append(score * EHD ** (-0.5))
    for score in scores:
        powers = jnp.exp(score - jnp.max(score, axis=-1, keepdims=True))
        weights.append((powers / jnp.sum(powers, axis=-1, keepdims=True)).astype(BF16))
    attn = [jnp.zeros((TILE_LEN, LANES), F32) for _ in range(tiles)]
    for span, inside, weight in zip(spans, insides, weights):
        part = jnp.where(inside, jnp.dot(weight, values[:, span], preferred_element_type=F32), 0.0)
        for t in range(span.start // LANES, span.stop // LANES):
            start = t * LANES - span.start
            attn[t] = attn[t] + part[:, start : start + LANES]
    return jnp.concatenate(attn, axis=1).astype(BF16)


def features_of(tile_ref, sent_ref, own_ref, other_ref, w_eo_ref):
    width, model = w_eo_ref.shape
    mine = rows_of(tile_ref)
    first, held = 3 * width // LANES, 2 * own_ref.shape[0]
    enc_x = [pick(t, mine, own_ref, other_ref) for t in range(first, held)]
    chunk = TILE_LEN // SUB
    last = sent_ref.shape[1] - held // (2 * SHARES)
    rest = first + model // LANES - held
    enc_x += [merge(sent_ref[pl.ds(tile_ref[0] * chunk, chunk), t]) for t in range(last - rest, last)]
    enc_x = jnp.concatenate(enc_x, axis=1).astype(F32)
    attn = attention_of(tile_ref, own_ref, other_ref, width)
    resid = enc_x + jnp.dot(attn, w_eo_ref[...], preferred_element_type=F32)
    center = resid - jnp.mean(resid, axis=-1, keepdims=True)
    spread = jnp.mean(center * center, axis=-1, keepdims=True)
    return (center * lax.rsqrt(spread + 1e-05)).astype(BF16)


def scores_kernel(query_ref, keys_ref, _, out_ref):
    slots, length, width = keys_ref.shape[0], keys_ref.shape[1], keys_ref.shape[2] // 2
    kv_heads = width // HD
    per = query_ref.shape[0] // kv_heads
    for g in range(kv_heads):
        keys = keys_ref[:, :, g * HD : (g + 1) * HD].reshape(slots * length, HD)
        rows = slice(g * per, (g + 1) * per)
        out_ref[rows, :] = lax.dot_general(
            query_ref[rows, :], keys, (((1,), (1,)), ((), ())), preferred_element_type=F32
        ) * HD ** (-0.5)


def attend_kernel(count_ref, query_ref, scores_ref, cache_ref, w_kv_ref, *refs):
    out_ref = refs[-1]
    slots, length, both = cache_ref.shape
    width = both // 2
    kv_heads = width // HD
    per = query_ref.shape[0] // kv_heads
    features = features_of(*refs[:-1])
    new_keys = jnp.dot(features, w_kv_ref[:, :width], preferred_element_type=F32).astype(BF16)
    scores = []
    for g in range(kv_heads):
        keys = new_keys[:, g * HD : (g + 1) * HD]
        head = query_ref[g * per : (g + 1) * per, :]
        scores.append(lax.dot_general(head, keys, (((1,), (1,)), ((), ())), preferred_element_type=F32))
    new_values = jnp.dot(features, w_kv_ref[:, width:], preferred_element_type=F32).astype(BF16)
    scores = jnp.concatenate(scores, axis=0) * HD ** (-0.5)
    slot = lax.broadcasted_iota(jnp.int32, scores_ref.shape, 1) // length
    old = jnp.where(slot < count_ref[0], scores_ref[...], -jnp.inf)
    scores = jnp.concatenate([old, scores], axis=1)
    powers = jnp.exp(scores - jnp.max(scores, axis=-1, keepdims=True))
    weights = (powers / jnp.sum(powers, axis=-1, keepdims=True)).astype(BF16)
    copies = out_ref.shape[0]
    halves = kv_heads // 2
    for g in range(kv_heads):
        mine = weights[g * per : (g + 1) * per]
        values = cache_ref[:, :, width + g * HD : width + (g + 1) * HD].reshape(slots * length, HD)
        part = jnp.dot(mine[:, : slots * length], values, preferred_element_type=F32)
        values = new_values[:, g * HD : (g + 1) * HD]
        part = part + jnp.dot(mine[:, slots * length :], values, preferred_element_type=F32)
        part = part.astype(BF16)
        for copy in range(g // halves, copies, 2):
            out_ref[copy, g % halves] = part


def finish_kernel(attn_ref, dec_x_ref, out_ref):
    attn = attn_ref[...].astype(F32)
    for k in range(attn.shape[0]):
        cols = slice(k * LANES, (k + 1) * LANES)
        out_ref[:, cols] = (dec_x_ref[:, cols].astype(F32) + attn[k : k + 1]).astype(BF16)


def finish_sums_kernel(sums_ref, dec_x_ref, out_ref, rows_ref, attn_ref):
    attn_ref[...] = add_halves(sums_ref, rows_ref)
    finish_kernel(attn_ref, dec_x_ref, out_ref)


def solution(mesh):
    devices = mesh.shape["seq"]
    swap = [(i, i ^ 1) for i in range(devices)]

    def exchange(sent):
        return lax.all_to_all(sent, "seq", 0, 0, tiled=True)

    def project(copies, weight, mate, *ready):
        depth, cols = weight.shape
        lanes = min(cols, LANES)
        sums = pl.pallas_call(
            project_kernel,
            out_shape=jax.ShapeDtypeStruct((devices, 2, cols // lanes, lanes), F32),
            in_specs=[VMEM] * 3 + [ANY] * len(ready),
            out_specs=VMEM,
            scratch_shapes=[pltpu.VMEM((devices * SUB, LANES), F32), pltpu.VMEM((devices, depth // 2), BF16)],
            compiler_params=params(8),
            cost_estimate=LONG,
        )(copies, weight, mate, *ready)
        return exchange(sums)

    def add_up(sums):
        sums = sums.reshape(devices // 2, 2, -1)
        return (sums[:, 0] + sums[:, 1]).astype(BF16).reshape(-1, LANES)

    def local(enc_x, enc_qkv, w_eo, w_kv, dec_x, w_q, w_o, cache_kv, doc_tile, cached_count):
        width = (enc_qkv.size + enc_x.size) // SUB
        spare = jnp.zeros((SUB, dec_x.shape[1] - width), BF16)
        rows_in = jnp.concatenate([enc_qkv.reshape(SUB, -1), enc_x, spare], axis=1)
        rows_in = jnp.concatenate([rows_in, dec_x], axis=0)
        w_q_mate = lax.ppermute(w_q, "seq", swap)
        w_o_mate = lax.ppermute(w_o, "seq", swap)
        blocks = (enc_qkv.size + enc_x.size) // (SUB * LANES)
        share = blocks // (2 * SHARES)
        rest = blocks - 2 * SHARES * share
        groups = dec_x.size // (2 * SUB * LANES) + rest + share
        rows = pltpu.VMEM((dec_x.shape[1] // LANES, LANES), F32)
        packed = pl.pallas_call(
            functools.partial(pack_kernel, width),
            out_shape=jax.ShapeDtypeStruct((devices, groups, SUB, LANES), BF16),
            in_specs=[VMEM],
            out_specs=VMEM,
            scratch_shapes=[rows],
            compiler_params=params(2),
            cost_estimate=LONG,
        )(rows_in)
        copies = exchange(packed)
        mine = pl.pallas_call(
            share_kernel,
            out_shape=jax.ShapeDtypeStruct((devices, share, SUB, LANES), BF16),
            in_specs=[VMEM],
            out_specs=VMEM,
            compiler_params=params(1),
        )(copies)
        shares = [lax.ppermute(mine, "seq", [(i, i ^ (2 * j)) for i in range(devices)]) for j in range(1, SHARES)]
        sums = project(copies, w_q, w_q_mate, w_o_mate)
        if sums.shape[-1] == LANES:
            query = pl.pallas_call(
                collect_kernel,
                out_shape=jax.ShapeDtypeStruct((sums.size // (2 * LANES), LANES), BF16),
                in_specs=[VMEM],
                out_specs=VMEM,
                scratch_shapes=[rows],
                compiler_params=params(1),
            )(sums)
        else:
            query = add_up(sums)
        merged = pl.pallas_call(
            merge_kernel,
            out_shape=jax.ShapeDtypeStruct((SHARES * share, devices * SUB, LANES), BF16),
            in_specs=[VMEM] * 5,
            out_specs=VMEM,
            compiler_params=params(4),
        )(query, mine, *shares)
        swapped = lax.ppermute(merged, "seq", swap)
        cache = cache_kv[0]
        scores = pl.pallas_call(
            scores_kernel,
            out_shape=jax.ShapeDtypeStruct((query.shape[0], cache.shape[0] * TILE_LEN), F32),
            in_specs=[VMEM] * 2 + [ANY],
            out_specs=VMEM,
            compiler_params=params(4),
        )(query, cache, merged)
        heads = query.shape[0]
        copies = pl.pallas_call(
            attend_kernel,
            out_shape=jax.ShapeDtypeStruct((devices, heads // (2 * SUB), SUB, LANES), BF16),
            in_specs=[SMEM] + [VMEM] * 4 + [SMEM] + [VMEM] * 4,
            out_specs=VMEM,
            compiler_params=params(16),
            cost_estimate=LONG,
        )(cached_count, query, scores, cache, w_kv, doc_tile, copies, merged, swapped, w_eo)
        sums = project(exchange(copies), w_o, w_o_mate)
        if sums.shape[-1] == LANES:
            kernel, scratch, attn = finish_sums_kernel, [rows, pltpu.VMEM((heads, LANES), BF16)], sums
        else:
            kernel, scratch, attn = finish_kernel, [], add_up(sums)
        return pl.pallas_call(
            kernel,
            out_shape=jax.ShapeDtypeStruct(dec_x.shape, BF16),
            in_specs=[VMEM] * 2,
            out_specs=VMEM,
            scratch_shapes=scratch,
            compiler_params=params(2),
            cost_estimate=LONG,
        )(attn, dec_x)

    return jax.shard_map(
        local,
        mesh=mesh,
        in_specs=(
            P(("group", "seq"), None),
            P(("group", "seq"), None, None),
            P(),
            P(),
            P(("group", "seq"), None),
            P(None, "seq"),
            P(None, "seq"),
            P(("group", "seq"), None, None, None),
            P(("group", "seq")),
            P(("group", "seq")),
        ),
        out_specs=P(("group", "seq"), None),
        check_vma=False,
    )
```

```python
import functools

import jax
import jax.numpy as jnp
from jax import lax
from jax.experimental import pallas as pl
from jax.experimental.pallas import tpu as pltpu
from jax.sharding import PartitionSpec as P

EH = 8
EHD = 80
HD = 128
TILE_LEN = 128
LANES = 128
SUB = 8
SHARES = 4
CHUNK = 512
VMEM = pl.BlockSpec(memory_space=pltpu.VMEM)
SMEM = pl.BlockSpec(memory_space=pltpu.SMEM)
ANY = pl.BlockSpec(memory_space=pl.ANY)
LONG = pl.CostEstimate(flops=10**10, transcendentals=0, bytes_accessed=10**7)
F32 = jnp.float32
BF16 = jnp.bfloat16


def params(mib):
    return pltpu.CompilerParams(vmem_limit_bytes=mib * 1024 * 1024)


def pack_kernel(width, rows_in_ref, out_ref, rows_ref):
    rows_in = rows_in_ref[...].astype(F32)
    x = rows_in[SUB : SUB + 1]
    scale = lax.rsqrt(jnp.mean(x * x, axis=-1, keepdims=True) + 1e-05)
    normed = x * scale
    groups = x.shape[1] // LANES
    for k in range(groups):
        rows_ref[k : k + 1, :] = normed[:, k * LANES : (k + 1) * LANES]
    copies = out_ref.shape[0]

    def put(place, block, to):
        block = block.astype(BF16)
        for copy in to:
            out_ref[copy, place] = block

    halves = groups // SUB // 2
    for i in range(2 * halves):
        put(i % halves, rows_ref[i * SUB : (i + 1) * SUB, :], range(i // halves, copies, 2))
    blocks = [rows_in[:SUB, t : t + LANES] for t in range(0, width, LANES)]
    share = len(blocks) // (2 * SHARES)
    for i, block in enumerate(blocks[2 * SHARES * share :]):
        put(halves + i, block, range(copies))
    first = out_ref.shape[1] - share
    for i, block in enumerate(blocks[: 2 * SHARES * share]):
        core, chip = divmod(i // share, SHARES)
        put(first + i % share, block, range(2 * chip + core, copies, 2 * SHARES))


def project_kernel(sent_ref, w_ref, mate_ref, *refs):
    out_ref, rows_ref, x_ref = refs[-3:]
    docs, half = x_ref.shape
    for i in range(half // (SUB * LANES)):
        rows_ref[...] = sent_ref[:, i].astype(F32).reshape(docs * SUB, LANES)
        for j in range(SUB):
            k = i * SUB + j
            x_ref[:, k * LANES : (k + 1) * LANES] = rows_ref[pl.ds(j, docs, stride=SUB), :].astype(BF16)
    core = lax.rem(lax.axis_index("seq"), 2)
    parts, lanes = out_ref.shape[2:]

    def multiply(side):
        for ref, place in ((w_ref, side), (mate_ref, 1 - side)):
            result = jnp.zeros((docs, ref.shape[1]), F32)
            for k in range(0, half, CHUNK):
                rows = slice(side * half + k, side * half + k + CHUNK)
                result += jnp.dot(x_ref[:, k : k + CHUNK], ref[rows, :], preferred_element_type=F32)
            result = jnp.stack([result[:, p * lanes : (p + 1) * lanes] for p in range(parts)], axis=1)
            out_ref[:, place] = result

    for side in range(2):
        pl.when(core == side)(functools.partial(multiply, side))


def add_halves(sums_ref, rows_ref):
    devices, cores, parts, _ = sums_ref.shape
    for chip in range(devices // 2):
        for core in range(cores):
            row = (chip * cores + core) * parts
            rows_ref[row : row + parts, :] = sums_ref[2 * chip, core] + sums_ref[2 * chip + 1, core]
    return rows_ref[...].astype(BF16)


def collect_kernel(sums_ref, out_ref, rows_ref):
    out_ref[...] = add_halves(sums_ref, rows_ref)


def share_kernel(own_ref, out_ref):
    share = out_ref.shape[1]
    out_ref[...] = own_ref[:, own_ref.shape[1] - share :]


def merge(block):
    return block.astype(F32).reshape(-1, LANES).astype(BF16)


def merge_kernel(query_ref, own_0, own_1, own_2, own_3, out_ref):
    share = out_ref.shape[0] // SHARES
    place = lax.rem(lax.axis_index("seq") // 2, SHARES)
    for j, ref in enumerate((own_0, own_1, own_2, own_3)):
        for i in range(share):
            out_ref[jnp.bitwise_xor(place, j) * share + i] = merge(ref[:, i])


def pick(place, rows, own_ref, other_ref):
    held = own_ref.shape[0]
    core = lax.rem(lax.axis_index("seq"), 2)
    side, index = divmod(place, held)
    return jnp.where(core == side, own_ref[index, rows], other_ref[index, rows])


def rows_of(tile_ref):
    return pl.ds(pl.multiple_of(tile_ref[0] * TILE_LEN, TILE_LEN), TILE_LEN)


def attention_of(tile_ref, own_ref, other_ref, width):
    tiles = width // LANES
    mine = rows_of(tile_ref)
    every = slice(None)
    query = jnp.concatenate([pick(t, mine, own_ref, other_ref) for t in range(tiles)], axis=1)
    keys = jnp.concatenate([pick(tiles + t, every, own_ref, other_ref) for t in range(tiles)], axis=1)
    values = jnp.concatenate([pick(2 * tiles + t, every, own_ref, other_ref) for t in range(tiles)], axis=1)
    column = lax.broadcasted_iota(jnp.int32, (TILE_LEN, width), 1)
    spans, insides, scores, weights = [], [], [], []
    for h in range(EH):
        span = slice(h * EHD // LANES * LANES, ((h + 1) * EHD - 1) // LANES * LANES + LANES)
        inside = (column[:, span] >= h * EHD) & (column[:, span] < (h + 1) * EHD)
        head = jnp.where(inside, query[:, span], jnp.zeros((), BF16))
        score = lax.dot_general(head, keys[:, span], (((1,), (1,)), ((), ())), preferred_element_type=F32)
        spans.append(span)
        insides.append(inside)
        scores.append(score * EHD ** (-0.5))
    for score in scores:
        powers = jnp.exp(score - jnp.max(score, axis=-1, keepdims=True))
        weights.append((powers / jnp.sum(powers, axis=-1, keepdims=True)).astype(BF16))
    attn = [jnp.zeros((TILE_LEN, LANES), F32) for _ in range(tiles)]
    for span, inside, weight in zip(spans, insides, weights):
        part = jnp.where(inside, jnp.dot(weight, values[:, span], preferred_element_type=F32), 0.0)
        for t in range(span.start // LANES, span.stop // LANES):
            start = t * LANES - span.start
            attn[t] = attn[t] + part[:, start : start + LANES]
    return jnp.concatenate(attn, axis=1).astype(BF16)


def features_of(tile_ref, sent_ref, own_ref, other_ref, w_eo_ref):
    width, model = w_eo_ref.shape
    mine = rows_of(tile_ref)
    first, held = 3 * width // LANES, 2 * own_ref.shape[0]
    enc_x = [pick(t, mine, own_ref, other_ref) for t in range(first, held)]
    chunk = TILE_LEN // SUB
    last = sent_ref.shape[1] - held // (2 * SHARES)
    rest = first + model // LANES - held
    enc_x += [merge(sent_ref[pl.ds(tile_ref[0] * chunk, chunk), t]) for t in range(last - rest, last)]
    enc_x = jnp.concatenate(enc_x, axis=1).astype(F32)
    attn = attention_of(tile_ref, own_ref, other_ref, width)
    resid = enc_x + jnp.dot(attn, w_eo_ref[...], preferred_element_type=F32)
    center = resid - jnp.mean(resid, axis=-1, keepdims=True)
    spread = jnp.mean(center * center, axis=-1, keepdims=True)
    return (center * lax.rsqrt(spread + 1e-05)).astype(BF16)


def scores_kernel(query_ref, keys_ref, _, out_ref):
    slots, length, width = keys_ref.shape[0], keys_ref.shape[1], keys_ref.shape[2] // 2
    kv_heads = width // HD
    per = query_ref.shape[0] // kv_heads
    query = query_ref[...]
    for g in range(kv_heads):
        keys = keys_ref[:, :, g * HD : (g + 1) * HD].reshape(slots * length, HD)
        rows = slice(g * per, (g + 1) * per)
        out_ref[rows, :] = lax.dot_general(
            query[rows], keys, (((1,), (1,)), ((), ())), preferred_element_type=F32
        ) * HD ** (-0.5)


def attend_kernel(count_ref, query_ref, scores_ref, cache_ref, w_kv_ref, *refs):
    out_ref = refs[-1]
    slots, length, both = cache_ref.shape
    width = both // 2
    kv_heads = width // HD
    per = query_ref.shape[0] // kv_heads
    query = query_ref[...]
    features = features_of(*refs[:-1])
    new_keys = jnp.dot(features, w_kv_ref[:, :width], preferred_element_type=F32).astype(BF16)
    scores = []
    for g in range(kv_heads):
        keys = new_keys[:, g * HD : (g + 1) * HD]
        head = query[g * per : (g + 1) * per]
        scores.append(lax.dot_general(head, keys, (((1,), (1,)), ((), ())), preferred_element_type=F32))
    new_values = jnp.dot(features, w_kv_ref[:, width:], preferred_element_type=F32).astype(BF16)
    scores = jnp.concatenate(scores, axis=0) * HD ** (-0.5)
    slot = lax.broadcasted_iota(jnp.int32, scores_ref.shape, 1) // length
    old = jnp.where(slot < count_ref[0], scores_ref[...], -jnp.inf)
    scores = jnp.concatenate([old, scores], axis=1)
    powers = jnp.exp(scores - jnp.max(scores, axis=-1, keepdims=True))
    weights = (powers / jnp.sum(powers, axis=-1, keepdims=True)).astype(BF16)
    copies = out_ref.shape[0]
    halves = kv_heads // 2
    for g in range(kv_heads):
        mine = weights[g * per : (g + 1) * per]
        values = cache_ref[:, :, width + g * HD : width + (g + 1) * HD].reshape(slots * length, HD)
        part = jnp.dot(mine[:, : slots * length], values, preferred_element_type=F32)
        values = new_values[:, g * HD : (g + 1) * HD]
        part = part + jnp.dot(mine[:, slots * length :], values, preferred_element_type=F32)
        part = part.astype(BF16)
        for copy in range(g // halves, copies, 2):
            out_ref[copy, g % halves] = part


def finish_kernel(attn_ref, dec_x_ref, out_ref):
    attn = attn_ref[...].astype(F32)
    for k in range(attn.shape[0]):
        cols = slice(k * LANES, (k + 1) * LANES)
        out_ref[:, cols] = (dec_x_ref[:, cols].astype(F32) + attn[k : k + 1]).astype(BF16)


def finish_sums_kernel(sums_ref, dec_x_ref, out_ref, rows_ref, attn_ref):
    attn_ref[...] = add_halves(sums_ref, rows_ref)
    finish_kernel(attn_ref, dec_x_ref, out_ref)


def solution(mesh):
    devices = mesh.shape["seq"]
    swap = [(i, i ^ 1) for i in range(devices)]

    def exchange(sent):
        return lax.all_to_all(sent, "seq", 0, 0, tiled=True)

    def project(copies, weight, mate, *ready):
        depth, cols = weight.shape
        lanes = min(cols, LANES)
        sums = pl.pallas_call(
            project_kernel,
            out_shape=jax.ShapeDtypeStruct((devices, 2, cols // lanes, lanes), F32),
            in_specs=[VMEM] * 3 + [ANY] * len(ready),
            out_specs=VMEM,
            scratch_shapes=[pltpu.VMEM((devices * SUB, LANES), F32), pltpu.VMEM((devices, depth // 2), BF16)],
            compiler_params=params(8),
            cost_estimate=LONG,
        )(copies, weight, mate, *ready)
        return exchange(sums)

    def add_up(sums):
        sums = sums.reshape(devices // 2, 2, -1)
        return (sums[:, 0] + sums[:, 1]).astype(BF16).reshape(-1, LANES)

    def local(enc_x, enc_qkv, w_eo, w_kv, dec_x, w_q, w_o, cache_kv, doc_tile, cached_count):
        width = (enc_qkv.size + enc_x.size) // SUB
        spare = jnp.zeros((SUB, dec_x.shape[1] - width), BF16)
        rows_in = jnp.concatenate([enc_qkv.reshape(SUB, -1), enc_x, spare], axis=1)
        rows_in = jnp.concatenate([rows_in, dec_x], axis=0)
        w_q_mate = lax.ppermute(w_q, "seq", swap)
        w_o_mate = lax.ppermute(w_o, "seq", swap)
        blocks = (enc_qkv.size + enc_x.size) // (SUB * LANES)
        share = blocks // (2 * SHARES)
        rest = blocks - 2 * SHARES * share
        groups = dec_x.size // (2 * SUB * LANES) + rest + share
        rows = pltpu.VMEM((dec_x.shape[1] // LANES, LANES), F32)
        packed = pl.pallas_call(
            functools.partial(pack_kernel, width),
            out_shape=jax.ShapeDtypeStruct((devices, groups, SUB, LANES), BF16),
            in_specs=[VMEM],
            out_specs=VMEM,
            scratch_shapes=[rows],
            compiler_params=params(2),
            cost_estimate=LONG,
        )(rows_in)
        copies = exchange(packed)
        mine = pl.pallas_call(
            share_kernel,
            out_shape=jax.ShapeDtypeStruct((devices, share, SUB, LANES), BF16),
            in_specs=[VMEM],
            out_specs=VMEM,
            compiler_params=params(1),
        )(copies)
        shares = [lax.ppermute(mine, "seq", [(i, i ^ (2 * j)) for i in range(devices)]) for j in range(1, SHARES)]
        sums = project(copies, w_q, w_q_mate, w_o_mate)
        if sums.shape[-1] == LANES:
            query = pl.pallas_call(
                collect_kernel,
                out_shape=jax.ShapeDtypeStruct((sums.size // (2 * LANES), LANES), BF16),
                in_specs=[VMEM],
                out_specs=VMEM,
                scratch_shapes=[rows],
                compiler_params=params(1),
            )(sums)
        else:
            query = add_up(sums)
        merged = pl.pallas_call(
            merge_kernel,
            out_shape=jax.ShapeDtypeStruct((SHARES * share, devices * SUB, LANES), BF16),
            in_specs=[VMEM] * 5,
            out_specs=VMEM,
            compiler_params=params(4),
        )(query, mine, *shares)
        swapped = lax.ppermute(merged, "seq", swap)
        cache = cache_kv[0]
        scores = pl.pallas_call(
            scores_kernel,
            out_shape=jax.ShapeDtypeStruct((query.shape[0], cache.shape[0] * TILE_LEN), F32),
            in_specs=[VMEM] * 2 + [ANY],
            out_specs=VMEM,
            compiler_params=params(4),
        )(query, cache, merged)
        heads = query.shape[0]
        copies = pl.pallas_call(
            attend_kernel,
            out_shape=jax.ShapeDtypeStruct((devices, heads // (2 * SUB), SUB, LANES), BF16),
            in_specs=[SMEM] + [VMEM] * 4 + [SMEM] + [VMEM] * 4,
            out_specs=VMEM,
            compiler_params=params(16),
            cost_estimate=LONG,
        )(cached_count, query, scores, cache, w_kv, doc_tile, copies, merged, swapped, w_eo)
        sums = project(exchange(copies), w_o, w_o_mate)
        if sums.shape[-1] == LANES:
            kernel, scratch, attn = finish_sums_kernel, [rows, pltpu.VMEM((heads, LANES), BF16)], sums
        else:
            kernel, scratch, attn = finish_kernel, [], add_up(sums)
        return pl.pallas_call(
            kernel,
            out_shape=jax.ShapeDtypeStruct(dec_x.shape, BF16),
            in_specs=[VMEM] * 2,
            out_specs=VMEM,
            scratch_shapes=scratch,
            compiler_params=params(2),
            cost_estimate=LONG,
        )(attn, dec_x)

    return jax.shard_map(
        local,
        mesh=mesh,
        in_specs=(
            P(("group", "seq"), None),
            P(("group", "seq"), None, None),
            P(),
            P(),
            P(("group", "seq"), None),
            P(None, "seq"),
            P(None, "seq"),
            P(("group", "seq"), None, None, None),
            P(("group", "seq")),
            P(("group", "seq")),
        ),
        out_specs=P(("group", "seq"), None),
        check_vma=False,
    )
```

```python
import functools

import jax
import jax.numpy as jnp
from jax import lax
from jax.experimental import pallas as pl
from jax.experimental.pallas import tpu as pltpu
from jax.sharding import PartitionSpec as P

EH = 8
EHD = 80
HD = 128
TILE_LEN = 128
LANES = 128
SUB = 8
SHARES = 4
CHUNK = 512
VMEM = pl.BlockSpec(memory_space=pltpu.VMEM)
SMEM = pl.BlockSpec(memory_space=pltpu.SMEM)
ANY = pl.BlockSpec(memory_space=pl.ANY)
LONG = pl.CostEstimate(flops=10**10, transcendentals=0, bytes_accessed=10**7)
F32 = jnp.float32
BF16 = jnp.bfloat16


def params(mib):
    return pltpu.CompilerParams(vmem_limit_bytes=mib * 1024 * 1024)


def pack_kernel(width, rows_in_ref, out_ref, last_ref, rows_ref):
    rows_in = rows_in_ref[...].astype(F32)
    x = rows_in[SUB : SUB + 1]
    scale = lax.rsqrt(jnp.mean(x * x, axis=-1, keepdims=True) + 1e-05)
    normed = x * scale
    groups = x.shape[1] // LANES
    for k in range(groups):
        rows_ref[k : k + 1, :] = normed[:, k * LANES : (k + 1) * LANES]
    copies = out_ref.shape[0]

    def put(place, block, to):
        block = block.astype(BF16)
        for copy in to:
            out_ref[copy, place] = block

    halves = groups // SUB // 2
    for i in range(2 * halves):
        put(i % halves, rows_ref[i * SUB : (i + 1) * SUB, :], range(i // halves, copies, 2))
    blocks = [rows_in[:SUB, t : t + LANES] for t in range(0, width, LANES)]
    share = len(blocks) // (2 * SHARES)
    last_ref[...] = blocks[-1]
    first = out_ref.shape[1] - share
    for i, block in enumerate(blocks[: 2 * SHARES * share]):
        core, chip = divmod(i // share, SHARES)
        put(first + i % share, block, range(2 * chip + core, copies, 2 * SHARES))


def project_kernel(sent_ref, w_ref, mate_ref, *refs):
    out_ref, rows_ref, x_ref, sums_ref = refs[-4:]
    docs, half = x_ref.shape
    for i in range(half // (SUB * LANES)):
        rows_ref[...] = sent_ref[:, i].astype(F32).reshape(docs * SUB, LANES)
        for j in range(SUB):
            k = i * SUB + j
            x_ref[:, k * LANES : (k + 1) * LANES] = rows_ref[pl.ds(j, docs, stride=SUB), :].astype(BF16)
    core = lax.rem(lax.axis_index("seq"), 2)
    cols = w_ref.shape[1]
    heads = 2 * cols // LANES

    def multiply(side):
        results = []
        for ref in (w_ref, mate_ref)[:: 1 - 2 * side]:
            result = jnp.zeros((docs, cols), F32)
            for k in range(0, half, CHUNK):
                rows = slice(side * half + k, side * half + k + CHUNK)
                result += jnp.dot(x_ref[:, k : k + CHUNK], ref[rows, :], preferred_element_type=F32)
            results.append(result)
        results = jnp.concatenate(results, axis=1)
        sums_ref[:, :heads] = jnp.stack([results[:, h * LANES : (h + 1) * LANES] for h in range(heads)], axis=1)

    for side in range(2):
        pl.when(core == side)(functools.partial(multiply, side))
    if len(refs) > 4:
        last = refs[0][...]
        for device in range(docs):
            start = device % 2 * (SUB // 2)
            sums_ref[device, heads:] = last[start : start + SUB // 2]
    out_ref[...] = sums_ref[...].astype(out_ref.dtype)


def add_halves(sums, rows_ref):
    heads = 2 * rows_ref.shape[0] // sums.shape[0]
    for chip in range(sums.shape[0] // 2):
        rows_ref[chip * heads : (chip + 1) * heads, :] = sums[2 * chip, :heads] + sums[2 * chip + 1, :heads]
    return rows_ref[...].astype(BF16)


def collect_kernel(sums_ref, out_ref, last_ref, rows_ref, tail_ref):
    sums = sums_ref[...].astype(F32)
    out_ref[...] = add_halves(sums, rows_ref)
    step = SUB // 2
    for device in range(sums.shape[0]):
        tail_ref[device * step : (device + 1) * step, :] = sums[device, sums.shape[1] - step :]
    last_ref[...] = tail_ref[...].astype(BF16)


def share_kernel(own_ref, out_ref):
    share = out_ref.shape[1]
    out_ref[...] = own_ref[:, own_ref.shape[1] - share :]


def merge(block):
    return block.astype(F32).reshape(-1, LANES).astype(BF16)


def merge_kernel(last_ref, own_0, own_1, own_2, own_3, out_ref):
    share = out_ref.shape[0] // SHARES
    place = lax.rem(lax.axis_index("seq") // 2, SHARES)
    for j, ref in enumerate((own_0, own_1, own_2, own_3)):
        for i in range(share):
            out_ref[jnp.bitwise_xor(place, j) * share + i] = merge(ref[:, i])
    out_ref[SHARES * share] = jnp.concatenate([last_ref[...], jnp.zeros(last_ref.shape, BF16)], axis=0)


def pick(place, rows, own_ref, other_ref):
    held = own_ref.shape[0] - 1
    core = lax.rem(lax.axis_index("seq"), 2)
    side, index = divmod(place, held)
    return jnp.where(core == side, own_ref[index, rows], other_ref[index, rows])


def rows_of(tile_ref):
    return pl.ds(pl.multiple_of(tile_ref[0] * TILE_LEN, TILE_LEN), TILE_LEN)


def attention_of(tile_ref, own_ref, other_ref, width):
    tiles = width // LANES
    mine = rows_of(tile_ref)
    every = slice(None)
    query = jnp.concatenate([pick(t, mine, own_ref, other_ref) for t in range(tiles)], axis=1)
    keys = jnp.concatenate([pick(tiles + t, every, own_ref, other_ref) for t in range(tiles)], axis=1)
    values = jnp.concatenate([pick(2 * tiles + t, every, own_ref, other_ref) for t in range(tiles)], axis=1)
    column = lax.broadcasted_iota(jnp.int32, (TILE_LEN, width), 1)
    spans, insides, scores, weights = [], [], [], []
    for h in range(EH):
        span = slice(h * EHD // LANES * LANES, ((h + 1) * EHD - 1) // LANES * LANES + LANES)
        inside = (column[:, span] >= h * EHD) & (column[:, span] < (h + 1) * EHD)
        head = jnp.where(inside, query[:, span], jnp.zeros((), BF16))
        score = lax.dot_general(head, keys[:, span], (((1,), (1,)), ((), ())), preferred_element_type=F32)
        spans.append(span)
        insides.append(inside)
        scores.append(score * EHD ** (-0.5))
    for score in scores:
        powers = jnp.exp(score - jnp.max(score, axis=-1, keepdims=True))
        weights.append((powers / jnp.sum(powers, axis=-1, keepdims=True)).astype(BF16))
    attn = [jnp.zeros((TILE_LEN, LANES), F32) for _ in range(tiles)]
    for span, inside, weight in zip(spans, insides, weights):
        part = jnp.where(inside, jnp.dot(weight, values[:, span], preferred_element_type=F32), 0.0)
        for t in range(span.start // LANES, span.stop // LANES):
            start = t * LANES - span.start
            attn[t] = attn[t] + part[:, start : start + LANES]
    return jnp.concatenate(attn, axis=1).astype(BF16)


def features_of(tile_ref, own_ref, other_ref, w_eo_ref, tail_ref):
    width, model = w_eo_ref.shape
    mine = rows_of(tile_ref)
    first, held = 3 * width // LANES, own_ref.shape[0] - 1
    enc_x = [pick(t, mine, own_ref, other_ref) for t in range(first, 2 * held)]
    half = TILE_LEN // 2
    rows = pl.ds(pl.multiple_of(tile_ref[0] * half, half), half)
    core = lax.rem(lax.axis_index("seq"), 2)
    for side in range(2):
        part = jnp.where(core == side, own_ref[held, rows], other_ref[held, rows]).astype(F32)
        step = SUB // 2
        for i in range(TILE_LEN // SUB):
            start = i * SUB + side * step
            tail_ref[start : start + step, :] = part[i * step : (i + 1) * step]
    enc_x.append(tail_ref[...].astype(BF16))
    enc_x = jnp.concatenate(enc_x, axis=1).astype(F32)
    attn = attention_of(tile_ref, own_ref, other_ref, width)
    resid = enc_x + jnp.dot(attn, w_eo_ref[...], preferred_element_type=F32)
    center = resid - jnp.mean(resid, axis=-1, keepdims=True)
    spread = jnp.mean(center * center, axis=-1, keepdims=True)
    return (center * lax.rsqrt(spread + 1e-05)).astype(BF16)


def scores_kernel(query_ref, keys_ref, _, out_ref):
    slots, length, width = keys_ref.shape[0], keys_ref.shape[1], keys_ref.shape[2] // 2
    kv_heads = width // HD
    per = query_ref.shape[0] // kv_heads
    query = query_ref[...]
    for g in range(kv_heads):
        keys = keys_ref[:, :, g * HD : (g + 1) * HD].reshape(slots * length, HD)
        rows = slice(g * per, (g + 1) * per)
        out_ref[rows, :] = lax.dot_general(
            query[rows], keys, (((1,), (1,)), ((), ())), preferred_element_type=F32
        ) * HD ** (-0.5)


def attend_kernel(count_ref, query_ref, scores_ref, cache_ref, w_kv_ref, *refs):
    out_ref, tail_ref = refs[-2:]
    slots, length, both = cache_ref.shape
    width = both // 2
    kv_heads = width // HD
    per = query_ref.shape[0] // kv_heads
    query = query_ref[...]
    features = features_of(*refs[:-2], tail_ref)
    new_keys = jnp.dot(features, w_kv_ref[:, :width], preferred_element_type=F32).astype(BF16)
    scores = []
    for g in range(kv_heads):
        keys = new_keys[:, g * HD : (g + 1) * HD]
        head = query[g * per : (g + 1) * per]
        scores.append(lax.dot_general(head, keys, (((1,), (1,)), ((), ())), preferred_element_type=F32))
    new_values = jnp.dot(features, w_kv_ref[:, width:], preferred_element_type=F32).astype(BF16)
    scores = jnp.concatenate(scores, axis=0) * HD ** (-0.5)
    slot = lax.broadcasted_iota(jnp.int32, scores_ref.shape, 1) // length
    old = jnp.where(slot < count_ref[0], scores_ref[...], -jnp.inf)
    scores = jnp.concatenate([old, scores], axis=1)
    powers = jnp.exp(scores - jnp.max(scores, axis=-1, keepdims=True))
    weights = (powers / jnp.sum(powers, axis=-1, keepdims=True)).astype(BF16)
    copies = out_ref.shape[0]
    halves = kv_heads // 2
    for g in range(kv_heads):
        mine = weights[g * per : (g + 1) * per]
        values = cache_ref[:, :, width + g * HD : width + (g + 1) * HD].reshape(slots * length, HD)
        part = jnp.dot(mine[:, : slots * length], values, preferred_element_type=F32)
        values = new_values[:, g * HD : (g + 1) * HD]
        part = part + jnp.dot(mine[:, slots * length :], values, preferred_element_type=F32)
        part = part.astype(BF16)
        for copy in range(g // halves, copies, 2):
            out_ref[copy, g % halves] = part


def finish_kernel(sums_ref, dec_x_ref, out_ref, rows_ref):
    attn = add_halves(sums_ref[...], rows_ref).astype(F32)
    for k in range(attn.shape[0]):
        cols = slice(k * LANES, (k + 1) * LANES)
        out_ref[:, cols] = (dec_x_ref[:, cols].astype(F32) + attn[k : k + 1]).astype(BF16)


def solution(mesh):
    devices = mesh.shape["seq"]
    swap = [(i, i ^ 1) for i in range(devices)]

    def exchange(sent):
        return lax.all_to_all(sent, "seq", 0, 0, tiled=True)

    def project(copies, weight, mate, *more):
        depth, cols = weight.shape
        shape = (devices, 2 * cols // LANES + (SUB // 2 if more else 0), LANES)
        sums = pl.pallas_call(
            project_kernel,
            out_shape=jax.ShapeDtypeStruct(shape, BF16 if more else F32),
            in_specs=[VMEM] * 3 + ([VMEM, ANY] if more else []),
            out_specs=VMEM,
            scratch_shapes=[
                pltpu.VMEM((devices * SUB, LANES), F32),
                pltpu.VMEM((devices, depth // 2), BF16),
                pltpu.VMEM(shape, F32),
            ],
            compiler_params=params(8),
            cost_estimate=LONG,
        )(copies, weight, mate, *more)
        return exchange(sums)

    def local(enc_x, enc_qkv, w_eo, w_kv, dec_x, w_q, w_o, cache_kv, doc_tile, cached_count):
        width = (enc_qkv.size + enc_x.size) // SUB
        spare = jnp.zeros((SUB, dec_x.shape[1] - width), BF16)
        rows_in = jnp.concatenate([enc_qkv.reshape(SUB, -1), enc_x, spare], axis=1)
        rows_in = jnp.concatenate([rows_in, dec_x], axis=0)
        w_q_mate = lax.ppermute(w_q, "seq", swap)
        w_o_mate = lax.ppermute(w_o, "seq", swap)
        blocks = (enc_qkv.size + enc_x.size) // (SUB * LANES)
        share = blocks // (2 * SHARES)
        groups = dec_x.size // (2 * SUB * LANES) + share
        rows = pltpu.VMEM((dec_x.shape[1] // LANES, LANES), F32)
        packed, last = pl.pallas_call(
            functools.partial(pack_kernel, width),
            out_shape=[
                jax.ShapeDtypeStruct((devices, groups, SUB, LANES), BF16),
                jax.ShapeDtypeStruct((SUB, LANES), F32),
            ],
            in_specs=[VMEM],
            out_specs=[VMEM] * 2,
            scratch_shapes=[rows],
            compiler_params=params(2),
            cost_estimate=LONG,
        )(rows_in)
        copies = exchange(packed)
        mine = pl.pallas_call(
            share_kernel,
            out_shape=jax.ShapeDtypeStruct((devices, share, SUB, LANES), BF16),
            in_specs=[VMEM],
            out_specs=VMEM,
            compiler_params=params(1),
        )(copies)
        shares = [lax.ppermute(mine, "seq", [(i, i ^ (2 * j)) for i in range(devices)]) for j in range(1, SHARES)]
        sums = project(copies, w_q, w_q_mate, last, w_o_mate)
        query, last = pl.pallas_call(
            collect_kernel,
            out_shape=[
                jax.ShapeDtypeStruct((dec_x.shape[1] // LANES, LANES), BF16),
                jax.ShapeDtypeStruct((devices * SUB // 2, LANES), BF16),
            ],
            in_specs=[VMEM],
            out_specs=[VMEM] * 2,
            scratch_shapes=[rows, pltpu.VMEM((devices * SUB // 2, LANES), F32)],
            compiler_params=params(1),
        )(sums)
        merged = pl.pallas_call(
            merge_kernel,
            out_shape=jax.ShapeDtypeStruct((SHARES * share + 1, devices * SUB, LANES), BF16),
            in_specs=[VMEM] * 5,
            out_specs=VMEM,
            compiler_params=params(4),
        )(last, mine, *shares)
        swapped = lax.ppermute(merged, "seq", swap)
        cache = cache_kv[0]
        scores = pl.pallas_call(
            scores_kernel,
            out_shape=jax.ShapeDtypeStruct((query.shape[0], cache.shape[0] * TILE_LEN), F32),
            in_specs=[VMEM] * 2 + [ANY],
            out_specs=VMEM,
            compiler_params=params(4),
        )(query, cache, merged)
        heads = query.shape[0]
        copies = pl.pallas_call(
            attend_kernel,
            out_shape=jax.ShapeDtypeStruct((devices, heads // (2 * SUB), SUB, LANES), BF16),
            in_specs=[SMEM] + [VMEM] * 4 + [SMEM] + [VMEM] * 3,
            out_specs=VMEM,
            scratch_shapes=[pltpu.VMEM((TILE_LEN, LANES), F32)],
            compiler_params=params(16),
            cost_estimate=LONG,
        )(cached_count, query, scores, cache, w_kv, doc_tile, merged, swapped, w_eo)
        sums = project(exchange(copies), w_o, w_o_mate)
        return pl.pallas_call(
            finish_kernel,
            out_shape=jax.ShapeDtypeStruct(dec_x.shape, BF16),
            in_specs=[VMEM] * 2,
            out_specs=VMEM,
            scratch_shapes=[rows],
            compiler_params=params(2),
            cost_estimate=LONG,
        )(sums, dec_x)

    return jax.shard_map(
        local,
        mesh=mesh,
        in_specs=(
            P(("group", "seq"), None),
            P(("group", "seq"), None, None),
            P(),
            P(),
            P(("group", "seq"), None),
            P(None, "seq"),
            P(None, "seq"),
            P(("group", "seq"), None, None, None),
            P(("group", "seq")),
            P(("group", "seq")),
        ),
        out_specs=P(("group", "seq"), None),
        check_vma=False,
    )
```

```python
import functools

import jax
import jax.numpy as jnp
from jax import lax
from jax.experimental import pallas as pl
from jax.experimental.pallas import tpu as pltpu
from jax.sharding import PartitionSpec as P

EH = 8
EHD = 80
HD = 128
TILE_LEN = 128
LANES = 128
SUB = 8
SHARES = 4
CHUNK = 512
VMEM = pl.BlockSpec(memory_space=pltpu.VMEM)
SMEM = pl.BlockSpec(memory_space=pltpu.SMEM)
ANY = pl.BlockSpec(memory_space=pl.ANY)
LONG = pl.CostEstimate(flops=10**10, transcendentals=0, bytes_accessed=10**7)
F32 = jnp.float32
BF16 = jnp.bfloat16


def params(mib):
    return pltpu.CompilerParams(vmem_limit_bytes=mib * 1024 * 1024)


def pack_kernel(width, rows_in_ref, out_ref, last_ref, rows_ref):
    rows_in = rows_in_ref[...].astype(F32)
    x = rows_in[SUB : SUB + 1]
    scale = lax.rsqrt(jnp.mean(x * x, axis=-1, keepdims=True) + 1e-05)
    normed = x * scale
    groups = x.shape[1] // LANES
    for k in range(groups):
        rows_ref[k : k + 1, :] = normed[:, k * LANES : (k + 1) * LANES]
    copies = out_ref.shape[0]

    def put(place, block, to):
        block = block.astype(BF16)
        for copy in to:
            out_ref[copy, place] = block

    halves = groups // SUB // 2
    for i in range(2 * halves):
        put(i % halves, rows_ref[i * SUB : (i + 1) * SUB, :], range(i // halves, copies, 2))
    blocks = [rows_in[:SUB, t : t + LANES] for t in range(0, width, LANES)]
    share = len(blocks) // (2 * SHARES)
    last_ref[...] = blocks[-1]
    first = out_ref.shape[1] - share
    for i, block in enumerate(blocks[: 2 * SHARES * share]):
        core, chip = divmod(i // share, SHARES)
        put(first + i % share, block, range(2 * chip + core, copies, 2 * SHARES))


def project_kernel(sent_ref, w_ref, mate_ref, *refs):
    out_ref, rows_ref, x_ref, sums_ref = refs[-4:]
    docs, half = x_ref.shape
    for i in range(half // (SUB * LANES)):
        rows_ref[...] = sent_ref[:, i].astype(F32).reshape(docs * SUB, LANES)
        for j in range(SUB):
            k = i * SUB + j
            x_ref[:, k * LANES : (k + 1) * LANES] = rows_ref[pl.ds(j, docs, stride=SUB), :].astype(BF16)
    core = lax.rem(lax.axis_index("seq"), 2)
    cols = w_ref.shape[1]
    heads = 2 * cols // LANES

    def multiply(side):
        results = []
        for ref in (w_ref, mate_ref)[:: 1 - 2 * side]:
            result = jnp.zeros((docs, cols), F32)
            for k in range(0, half, CHUNK):
                rows = slice(side * half + k, side * half + k + CHUNK)
                result += jnp.dot(x_ref[:, k : k + CHUNK], ref[rows, :], preferred_element_type=F32)
            results.append(result)
        results = jnp.concatenate(results, axis=1)
        sums_ref[...] = jnp.stack([results[:, h * LANES : (h + 1) * LANES] for h in range(heads)], axis=1)

    for side in range(2):
        pl.when(core == side)(functools.partial(multiply, side))
    if len(refs) == 4:
        out_ref[...] = sums_ref[...]
        return
    sums = sums_ref[...]
    high = sums.astype(BF16)
    out_ref[:, 0, :heads] = high
    out_ref[:, 1, :heads] = (sums - high.astype(F32)).astype(BF16)
    last = refs[0][...].astype(BF16)
    for device in range(docs):
        start = device % 2 * (SUB // 2)
        out_ref[device, 2] = last[start : start + SUB // 2]


def add_halves(sums, rows_ref):
    heads = 2 * rows_ref.shape[0] // sums.shape[0]
    for chip in range(sums.shape[0] // 2):
        rows_ref[chip * heads : (chip + 1) * heads, :] = sums[2 * chip, :heads] + sums[2 * chip + 1, :heads]
    return rows_ref[...].astype(BF16)


def collect_kernel(sums_ref, out_ref, last_ref, rows_ref, tail_ref):
    sums = sums_ref[:, 0].astype(F32) + sums_ref[:, 1].astype(F32)
    out_ref[...] = add_halves(sums, rows_ref)
    step = SUB // 2
    last = sums_ref[:, 2].astype(F32)
    for device in range(last.shape[0]):
        tail_ref[device * step : (device + 1) * step, :] = last[device]
    last_ref[...] = tail_ref[...].astype(BF16)


def share_kernel(own_ref, out_ref):
    share = out_ref.shape[1]
    out_ref[...] = own_ref[:, own_ref.shape[1] - share :]


def merge(block):
    return block.astype(F32).reshape(-1, LANES).astype(BF16)


def merge_kernel(last_ref, own_0, own_1, own_2, own_3, out_ref):
    share = out_ref.shape[0] // SHARES
    place = lax.rem(lax.axis_index("seq") // 2, SHARES)
    for j, ref in enumerate((own_0, own_1, own_2, own_3)):
        for i in range(share):
            out_ref[jnp.bitwise_xor(place, j) * share + i] = merge(ref[:, i])
    out_ref[SHARES * share] = jnp.concatenate([last_ref[...], jnp.zeros(last_ref.shape, BF16)], axis=0)


def pick(place, rows, own_ref, other_ref):
    held = own_ref.shape[0] - 1
    core = lax.rem(lax.axis_index("seq"), 2)
    side, index = divmod(place, held)
    return jnp.where(core == side, own_ref[index, rows], other_ref[index, rows])


def rows_of(tile_ref):
    return pl.ds(pl.multiple_of(tile_ref[0] * TILE_LEN, TILE_LEN), TILE_LEN)


def attention_of(tile_ref, own_ref, other_ref, width):
    tiles = width // LANES
    mine = rows_of(tile_ref)
    every = slice(None)
    query = jnp.concatenate([pick(t, mine, own_ref, other_ref) for t in range(tiles)], axis=1)
    keys = jnp.concatenate([pick(tiles + t, every, own_ref, other_ref) for t in range(tiles)], axis=1)
    values = jnp.concatenate([pick(2 * tiles + t, every, own_ref, other_ref) for t in range(tiles)], axis=1)
    column = lax.broadcasted_iota(jnp.int32, (TILE_LEN, width), 1)
    spans, insides, scores, weights = [], [], [], []
    for h in range(EH):
        span = slice(h * EHD // LANES * LANES, ((h + 1) * EHD - 1) // LANES * LANES + LANES)
        inside = (column[:, span] >= h * EHD) & (column[:, span] < (h + 1) * EHD)
        head = jnp.where(inside, query[:, span], jnp.zeros((), BF16))
        score = lax.dot_general(head, keys[:, span], (((1,), (1,)), ((), ())), preferred_element_type=F32)
        spans.append(span)
        insides.append(inside)
        scores.append(score * EHD ** (-0.5))
    for score in scores:
        powers = jnp.exp(score - jnp.max(score, axis=-1, keepdims=True))
        weights.append((powers / jnp.sum(powers, axis=-1, keepdims=True)).astype(BF16))
    attn = [jnp.zeros((TILE_LEN, LANES), F32) for _ in range(tiles)]
    for span, inside, weight in zip(spans, insides, weights):
        part = jnp.where(inside, jnp.dot(weight, values[:, span], preferred_element_type=F32), 0.0)
        for t in range(span.start // LANES, span.stop // LANES):
            start = t * LANES - span.start
            attn[t] = attn[t] + part[:, start : start + LANES]
    return jnp.concatenate(attn, axis=1).astype(BF16)


def features_of(tile_ref, own_ref, other_ref, w_eo_ref, tail_ref):
    width, model = w_eo_ref.shape
    mine = rows_of(tile_ref)
    first, held = 3 * width // LANES, own_ref.shape[0] - 1
    enc_x = [pick(t, mine, own_ref, other_ref) for t in range(first, 2 * held)]
    half = TILE_LEN // 2
    rows = pl.ds(pl.multiple_of(tile_ref[0] * half, half), half)
    core = lax.rem(lax.axis_index("seq"), 2)
    for side in range(2):
        part = jnp.where(core == side, own_ref[held, rows], other_ref[held, rows]).astype(F32)
        step = SUB // 2
        for i in range(TILE_LEN // SUB):
            start = i * SUB + side * step
            tail_ref[start : start + step, :] = part[i * step : (i + 1) * step]
    enc_x.append(tail_ref[...].astype(BF16))
    enc_x = jnp.concatenate(enc_x, axis=1).astype(F32)
    attn = attention_of(tile_ref, own_ref, other_ref, width)
    resid = enc_x + jnp.dot(attn, w_eo_ref[...], preferred_element_type=F32)
    center = resid - jnp.mean(resid, axis=-1, keepdims=True)
    spread = jnp.mean(center * center, axis=-1, keepdims=True)
    return (center * lax.rsqrt(spread + 1e-05)).astype(BF16)


def scores_kernel(query_ref, keys_ref, _, out_ref):
    slots, length, width = keys_ref.shape[0], keys_ref.shape[1], keys_ref.shape[2] // 2
    kv_heads = width // HD
    per = query_ref.shape[0] // kv_heads
    query = query_ref[...]
    for g in range(kv_heads):
        keys = keys_ref[:, :, g * HD : (g + 1) * HD].reshape(slots * length, HD)
        rows = slice(g * per, (g + 1) * per)
        out_ref[rows, :] = lax.dot_general(
            query[rows], keys, (((1,), (1,)), ((), ())), preferred_element_type=F32
        ) * HD ** (-0.5)


def attend_kernel(count_ref, query_ref, scores_ref, cache_ref, w_kv_ref, *refs):
    out_ref, tail_ref = refs[-2:]
    slots, length, both = cache_ref.shape
    width = both // 2
    kv_heads = width // HD
    per = query_ref.shape[0] // kv_heads
    query = query_ref[...]
    features = features_of(*refs[:-2], tail_ref)
    new_keys = jnp.dot(features, w_kv_ref[:, :width], preferred_element_type=F32).astype(BF16)
    scores = []
    for g in range(kv_heads):
        keys = new_keys[:, g * HD : (g + 1) * HD]
        head = query[g * per : (g + 1) * per]
        scores.append(lax.dot_general(head, keys, (((1,), (1,)), ((), ())), preferred_element_type=F32))
    new_values = jnp.dot(features, w_kv_ref[:, width:], preferred_element_type=F32).astype(BF16)
    scores = jnp.concatenate(scores, axis=0) * HD ** (-0.5)
    slot = lax.broadcasted_iota(jnp.int32, scores_ref.shape, 1) // length
    old = jnp.where(slot < count_ref[0], scores_ref[...], -jnp.inf)
    scores = jnp.concatenate([old, scores], axis=1)
    powers = jnp.exp(scores - jnp.max(scores, axis=-1, keepdims=True))
    weights = (powers / jnp.sum(powers, axis=-1, keepdims=True)).astype(BF16)
    copies = out_ref.shape[0]
    halves = kv_heads // 2
    for g in range(kv_heads):
        mine = weights[g * per : (g + 1) * per]
        values = cache_ref[:, :, width + g * HD : width + (g + 1) * HD].reshape(slots * length, HD)
        part = jnp.dot(mine[:, : slots * length], values, preferred_element_type=F32)
        values = new_values[:, g * HD : (g + 1) * HD]
        part = part + jnp.dot(mine[:, slots * length :], values, preferred_element_type=F32)
        part = part.astype(BF16)
        for copy in range(g // halves, copies, 2):
            out_ref[copy, g % halves] = part


def finish_kernel(sums_ref, dec_x_ref, out_ref, rows_ref):
    attn = add_halves(sums_ref[...], rows_ref).astype(F32)
    for k in range(attn.shape[0]):
        cols = slice(k * LANES, (k + 1) * LANES)
        out_ref[:, cols] = (dec_x_ref[:, cols].astype(F32) + attn[k : k + 1]).astype(BF16)


def solution(mesh):
    devices = mesh.shape["seq"]
    swap = [(i, i ^ 1) for i in range(devices)]

    def exchange(sent):
        return lax.all_to_all(sent, "seq", 0, 0, tiled=True)

    def project(copies, weight, mate, *more):
        depth, cols = weight.shape
        shape = (devices, 2 * cols // LANES, LANES)
        sums = pl.pallas_call(
            project_kernel,
            out_shape=jax.ShapeDtypeStruct((devices, 3, SUB // 2, LANES) if more else shape, BF16 if more else F32),
            in_specs=[VMEM] * 3 + ([VMEM, ANY] if more else []),
            out_specs=VMEM,
            scratch_shapes=[
                pltpu.VMEM((devices * SUB, LANES), F32),
                pltpu.VMEM((devices, depth // 2), BF16),
                pltpu.VMEM(shape, F32),
            ],
            compiler_params=params(8),
            cost_estimate=LONG,
        )(copies, weight, mate, *more)
        return exchange(sums)

    def local(enc_x, enc_qkv, w_eo, w_kv, dec_x, w_q, w_o, cache_kv, doc_tile, cached_count):
        width = (enc_qkv.size + enc_x.size) // SUB
        spare = jnp.zeros((SUB, dec_x.shape[1] - width), BF16)
        rows_in = jnp.concatenate([enc_qkv.reshape(SUB, -1), enc_x, spare], axis=1)
        rows_in = jnp.concatenate([rows_in, dec_x], axis=0)
        w_q_mate = lax.ppermute(w_q, "seq", swap)
        w_o_mate = lax.ppermute(w_o, "seq", swap)
        blocks = (enc_qkv.size + enc_x.size) // (SUB * LANES)
        share = blocks // (2 * SHARES)
        groups = dec_x.size // (2 * SUB * LANES) + share
        rows = pltpu.VMEM((dec_x.shape[1] // LANES, LANES), F32)
        packed, last = pl.pallas_call(
            functools.partial(pack_kernel, width),
            out_shape=[
                jax.ShapeDtypeStruct((devices, groups, SUB, LANES), BF16),
                jax.ShapeDtypeStruct((SUB, LANES), F32),
            ],
            in_specs=[VMEM],
            out_specs=[VMEM] * 2,
            scratch_shapes=[rows],
            compiler_params=params(2),
            cost_estimate=LONG,
        )(rows_in)
        copies = exchange(packed)
        mine = pl.pallas_call(
            share_kernel,
            out_shape=jax.ShapeDtypeStruct((devices, share, SUB, LANES), BF16),
            in_specs=[VMEM],
            out_specs=VMEM,
            compiler_params=params(1),
        )(copies)
        shares = [lax.ppermute(mine, "seq", [(i, i ^ (2 * j)) for i in range(devices)]) for j in range(1, SHARES)]
        sums = project(copies, w_q, w_q_mate, last, w_o_mate)
        query, last = pl.pallas_call(
            collect_kernel,
            out_shape=[
                jax.ShapeDtypeStruct((dec_x.shape[1] // LANES, LANES), BF16),
                jax.ShapeDtypeStruct((devices * SUB // 2, LANES), BF16),
            ],
            in_specs=[VMEM],
            out_specs=[VMEM] * 2,
            scratch_shapes=[rows, pltpu.VMEM((devices * SUB // 2, LANES), F32)],
            compiler_params=params(1),
        )(sums)
        merged = pl.pallas_call(
            merge_kernel,
            out_shape=jax.ShapeDtypeStruct((SHARES * share + 1, devices * SUB, LANES), BF16),
            in_specs=[VMEM] * 5,
            out_specs=VMEM,
            compiler_params=params(4),
        )(last, mine, *shares)
        swapped = lax.ppermute(merged, "seq", swap)
        cache = cache_kv[0]
        scores = pl.pallas_call(
            scores_kernel,
            out_shape=jax.ShapeDtypeStruct((query.shape[0], cache.shape[0] * TILE_LEN), F32),
            in_specs=[VMEM] * 2 + [ANY],
            out_specs=VMEM,
            compiler_params=params(4),
        )(query, cache, merged)
        heads = query.shape[0]
        copies = pl.pallas_call(
            attend_kernel,
            out_shape=jax.ShapeDtypeStruct((devices, heads // (2 * SUB), SUB, LANES), BF16),
            in_specs=[SMEM] + [VMEM] * 4 + [SMEM] + [VMEM] * 3,
            out_specs=VMEM,
            scratch_shapes=[pltpu.VMEM((TILE_LEN, LANES), F32)],
            compiler_params=params(16),
            cost_estimate=LONG,
        )(cached_count, query, scores, cache, w_kv, doc_tile, merged, swapped, w_eo)
        sums = project(exchange(copies), w_o, w_o_mate)
        return pl.pallas_call(
            finish_kernel,
            out_shape=jax.ShapeDtypeStruct(dec_x.shape, BF16),
            in_specs=[VMEM] * 2,
            out_specs=VMEM,
            scratch_shapes=[rows],
            compiler_params=params(2),
            cost_estimate=LONG,
        )(sums, dec_x)

    return jax.shard_map(
        local,
        mesh=mesh,
        in_specs=(
            P(("group", "seq"), None),
            P(("group", "seq"), None, None),
            P(),
            P(),
            P(("group", "seq"), None),
            P(None, "seq"),
            P(None, "seq"),
            P(("group", "seq"), None, None, None),
            P(("group", "seq")),
            P(("group", "seq")),
        ),
        out_specs=P(("group", "seq"), None),
        check_vma=False,
    )
```
